512 devices in a mesh: group: 8 (over x_hi, y), ctx: 64 (over z, x_lo, core).
Axes of the slice: x: 4 (x_hi: 2, x_lo: 2; x = x_hi * 2 + x_lo), y: 4, z: 16, core: 2. Of those that a mesh axis runs over, the one named last changes fastest.
Arguments:
- queries: bfloat16 [11264, 2048], P('ctx', 'group'), may hold values from -30 to 30
- key_rows: bfloat16 [11264, 2048], P('ctx', 'group'), may hold values from -30 to 30
- value_rows: bfloat16 [11264, 2048], P('ctx', 'group'), may hold values from -6 to 6
- query_dir: bfloat16 [11264, 2048], P('ctx', 'group'), may hold values from -12 to 12
- out_weight: bfloat16 [2048, 3072], P('group'), may hold values from -0.125 to 0.125
Outputs:
- query_next: float32 [11264, 2048], P('ctx', 'group')
The draws below stay inside these ranges and needn't reach their ends.
All inputs are finite; a program needn't handle non-finite values.
Results may differ from the reference program's by a relative error of at most 0.017.
Values may be sent and summed in bfloat16 or wider, within the bound.
A program may use at most 128 MiB of HBM per device.

```python
import jax
import jax.numpy as jnp
from jax import lax

D = 3072
HEADS = 16
HEAD_DIM = 128
TOKENS = 11264


def draw_queries(key, part):
    key = jax.random.fold_in(key, 7)
    sample = jax.random.normal(key, (TOKENS, HEADS * HEAD_DIM), jnp.float32)
    return jnp.clip(sample, -30.0, 30.0).astype(jnp.bfloat16)


def draw_key_rows(key, part):
    key = jax.random.fold_in(key, 13)
    sample = jax.random.normal(key, (TOKENS, HEADS * HEAD_DIM), jnp.float32)
    return jnp.clip(sample, -30.0, 30.0).astype(jnp.bfloat16)


def draw_query_dir(key, part):
    key = jax.random.fold_in(key, 19)
    rising = 0.6 + 0.6 * jnp.arange(TOKENS, dtype=jnp.float32)[:, None] / TOKENS
    sample = jax.random.normal(key, (TOKENS, HEADS * HEAD_DIM), jnp.float32) * rising
    return jnp.clip(sample, -12.0, 12.0).astype(jnp.bfloat16)


def level_of(key, dims, cuts, smallest, largest):
    loudness, own = 1.0, jax.random.fold_in(key, 6)
    for dim, parts in cuts:
        steps = jnp.exp(jax.random.uniform(jax.random.fold_in(own, dim), (parts,), jnp.float32, smallest / len(cuts), largest / len(cuts)))
        loudness = loudness * jnp.repeat(steps, dims[dim] // parts).reshape([-1 if axis == dim else 1 for axis in range(len(dims))])
    return loudness


def gaussian(own_key, shape, deviation, bound, split=(), held_as=jnp.bfloat16):
    drawn = deviation * jax.random.normal(own_key, shape, jnp.float32)
    if split:
        drawn = drawn * level_of(own_key, shape, split, -0.22, 0.18)
    return jnp.clip(drawn, -bound, bound).astype(held_as)


def setup_inputs(seed: int = 0) -> dict:
    key_list = jax.random.split(jax.random.key(seed), 6)
    queries = draw_queries(jax.random.fold_in(key_list[5], 71), 0)
    key_rows = draw_key_rows(jax.random.fold_in(key_list[5], 71), 0)
    value_rows = gaussian(key_list[2], (TOKENS, HEADS * HEAD_DIM), 1.0, 6.0, ((0, 64), (1, 8)))
    query_dir = draw_query_dir(jax.random.fold_in(key_list[5], 71), 0)
    out_weight = gaussian(key_list[4], (HEADS * HEAD_DIM, D), (HEADS * HEAD_DIM) ** -0.5, 0.125, ((0, 8),))
    return {"queries": queries, "key_rows": key_rows, "value_rows": value_rows, "query_dir": query_dir, "out_weight": out_weight}


def split_heads(matrix):
    return matrix.reshape(TOKENS, HEADS, HEAD_DIM).transpose(1, 0, 2)


def join_heads(stacked):
    return stacked.transpose(1, 0, 2).reshape(TOKENS, HEADS * HEAD_DIM)


def forward_head(inputs):
    queries, key_rows, value_rows, query_dir = inputs
    scaling = HEAD_DIM ** -0.5
    scores = jnp.dot(queries, key_rows.T, preferred_element_type=jnp.float32) * scaling
    highest = jnp.max(scores, axis=1, keepdims=True)
    weights = jnp.exp(scores - highest)
    totals = jnp.sum(weights, axis=1, keepdims=True)
    tangent_scores = jnp.dot(query_dir, key_rows.T, preferred_element_type=jnp.float32) * scaling
    weighted = weights * tangent_scores
    rounded = weights.astype(jnp.bfloat16)
    mixed_sum = jnp.dot(rounded, value_rows, preferred_element_type=jnp.float32)
    tangent_mixed = jnp.dot(weighted.astype(jnp.bfloat16), value_rows, preferred_element_type=jnp.float32)
    attended = mixed_sum / totals
    tangent = tangent_mixed / totals - (jnp.sum(weighted, axis=1, keepdims=True) / totals) * attended
    log_total = highest[:, 0] + jnp.log(totals[:, 0])
    return attended, tangent.astype(jnp.bfloat16), log_total


def backward_head(inputs):
    queries, key_rows, value_rows, cotangent, log_total, centering = inputs
    scaling = HEAD_DIM ** -0.5
    scores = jnp.dot(queries, key_rows.T, preferred_element_type=jnp.float32) * scaling
    probabilities = jnp.exp(scores - log_total[:, None])
    back_scores = jnp.dot(cotangent, value_rows.T, preferred_element_type=jnp.float32)
    score_grad = probabilities * (back_scores - centering[:, None])
    return jnp.dot(score_grad.astype(jnp.bfloat16), key_rows, preferred_element_type=jnp.float32) * scaling


def reference(queries, key_rows, value_rows, query_dir, out_weight):
    stacked = (split_heads(queries), split_heads(key_rows), split_heads(value_rows))
    attended, tangent, log_total = lax.map(forward_head, stacked + (split_heads(query_dir),))
    projected = jnp.dot(join_heads(tangent), out_weight, preferred_element_type=jnp.float32)
    curvature = jnp.sum(projected * projected)
    cotangent = jnp.dot(projected.astype(jnp.bfloat16), out_weight.T, preferred_element_type=jnp.float32).astype(jnp.bfloat16)
    cotangent_heads = split_heads(cotangent)
    centering = jnp.sum(cotangent_heads.astype(jnp.float32) * attended, axis=2)
    query_grad = lax.map(backward_head, stacked + (cotangent_heads, log_total, centering))
    dir_float = query_dir.astype(jnp.float32)
    residual_sq = jnp.sum(dir_float * dir_float)
    step_size = residual_sq / curvature
    return dir_float - step_size * join_heads(query_grad)
```

```python
import functools
import math

import jax
import jax.numpy as jnp
from jax import lax
from jax.experimental import pallas as pl
from jax.experimental.pallas import tpu as pltpu
from jax.sharding import PartitionSpec as P

MESH = pl.DeviceIdType.MESH
HEAD_DIM = 128
SCALING = HEAD_DIM ** (-0.5)
EXP2_SCALE = SCALING * math.log2(math.e)
N_Y, N_XLO, N_CORE = 4, 2, 2
WINDOW = 48
F32, BF16 = jnp.float32, jnp.bfloat16


def dot_nt(a, b):
    return lax.dot_general(a, b, (((1,), (1,)), ((), ())), preferred_element_type=F32)


def dot_nn(a, b):
    return lax.dot_general(a, b, (((1,), (0,)), ((), ())), preferred_element_type=F32)


def kernel(
    n_group, n_z, rows,
    q_ref, k_ref, v_ref, d_ref, w_ref, out_ref,
    kv, qd, pw, highs, high, acc, dirb, att, tbuf, tin, wbuf, plow, cout, cin, cbuf, qg, qg_in,
    red_z, red_g, red_c,
    local_sem, swap_send, swap_recv, ring_send, ring_recv, sib_send, sib_recv,
    w_send, w_recv, t_send, t_recv, c_send, c_recv, red_send, red_recv, back_send, back_recv,
):
    group, ctx = lax.axis_index("group"), lax.axis_index("ctx")
    x_hi, y = lax.div(group, N_Y), lax.rem(group, N_Y)
    z, x_lo, core = lax.div(ctx, 4), lax.rem(lax.div(ctx, 2), 2), lax.rem(ctx, 2)
    head = 2 * group + x_lo
    both = 2 * rows
    unit = 4 * rows
    half_z = n_z // 2
    n_heads = 2 * n_group
    wide = wbuf.shape[1]

    def at_ctx(z_, x_lo_, core_):
        return 4 * z_ + 2 * x_lo_ + core_

    z_next, z_prev = lax.rem(z + 1, n_z), lax.rem(z + n_z - 1, n_z)
    dev_next = (group, at_ctx(z_next, x_lo, core))
    dev_prev = (group, at_ctx(z_prev, x_lo, core))
    dev_sib = (group, at_ctx(z, x_lo, 1 - core))
    dev_pair = (group, at_ctx(z, 1 - x_lo, core))
    dev_across = ((1 - x_hi) * N_Y + y, at_ctx(z, 1 - x_lo, core))
    y_next, y_prev = lax.rem(y + 1, N_Y), lax.rem(y + N_Y - 1, N_Y)
    dev_up = (x_hi * N_Y + y_next, ctx)
    dev_down = (x_hi * N_Y + y_prev, ctx)

    def remote(src, dst, send, recv, device):
        return pltpu.make_async_remote_copy(
            src_ref=src, dst_ref=dst, send_sem=send, recv_sem=recv,
            device_id=device, device_id_type=MESH,
        )

    def part_of(o):
        return x_lo + o - 2 * x_lo * o

    def chunk_rows(p, core_, j):
        start = lax.div(p, 2) * (2 * unit) + j * unit + lax.rem(p, 2) * both + core_ * rows
        return pl.ds(pl.multiple_of(start, 16), rows)

    def chunk(p, core_, j):
        return kv.at[chunk_rows(p, core_, j)]

    own_cols = pl.ds(pl.multiple_of(x_lo * HEAD_DIM, HEAD_DIM), HEAD_DIM)
    other_cols = pl.ds(pl.multiple_of((1 - x_lo) * HEAD_DIM, HEAD_DIM), HEAD_DIM)
    own_rows = pl.ds(pl.multiple_of(x_lo * rows, 16), rows)
    other_rows = pl.ds(pl.multiple_of((1 - x_lo) * rows, 16), rows)
    own_tan = pl.ds(pl.multiple_of(both + x_lo * rows, 16), rows)
    other_tan = pl.ds(pl.multiple_of(both + (1 - x_lo) * rows, 16), rows)
    first = chunk_rows(0, core, x_lo)
    second = chunk_rows(0, core, 1 - x_lo)
    own_half = pl.ds(pl.multiple_of(x_lo * wide, 128), wide)
    other_half = pl.ds(pl.multiple_of((1 - x_lo) * wide, 128), wide)

    def w_rows(x_hi_, y_, piece):
        start = (x_hi_ * N_Y + y_) * 256 + piece * 128
        return pl.ds(pl.multiple_of(start, 128), 128)

    local = [
        pltpu.make_async_copy(k_ref.at[:, own_cols], kv.at[first, 0:HEAD_DIM], local_sem.at[0]),
        pltpu.make_async_copy(
            v_ref.at[:, own_cols], kv.at[first, HEAD_DIM : 2 * HEAD_DIM], local_sem.at[1]
        ),
        pltpu.make_async_copy(q_ref.at[:, own_cols], qd.at[own_rows], local_sem.at[2]),
        pltpu.make_async_copy(d_ref.at[:, own_cols], qd.at[own_tan], local_sem.at[3]),
        pltpu.make_async_copy(d_ref, dirb, local_sem.at[4]),
        pltpu.make_async_copy(
            w_ref.at[:, own_half],
            wbuf.at[pl.ds(pl.multiple_of(group * 256, 256), 256)],
            local_sem.at[5],
        ),
    ]
    for copy in local:
        copy.start()

    barrier = pltpu.get_barrier_semaphore()

    def greet(device):
        pl.semaphore_signal(barrier, inc=1, device_id=device, device_id_type=MESH)

    @pl.loop(1, n_z)
    def _(i):
        greet((group, at_ctx(lax.rem(z + i, n_z), x_lo, core)))

    @pl.loop(1, n_group)
    def _(i):
        other = lax.rem(group + i, n_group)
        greet((other, at_ctx(z, x_lo, core)))
        greet((other, at_ctx(z, 1 - x_lo, core)))

    greet(dev_pair)
    greet(dev_sib)
    greet((group, at_ctx(z, 1 - x_lo, 1 - core)))
    pl.semaphore_wait(barrier, n_z - 1 + 2 * (n_group - 1) + 3)

    swap = [
        remote(
            k_ref.at[:, other_cols], kv.at[first, 0:HEAD_DIM],
            swap_send.at[0], swap_recv.at[0], dev_pair,
        ),
        remote(
            v_ref.at[:, other_cols], kv.at[first, HEAD_DIM : 2 * HEAD_DIM],
            swap_send.at[1], swap_recv.at[1], dev_pair,
        ),
        remote(
            q_ref.at[:, other_cols], qd.at[own_rows], swap_send.at[2], swap_recv.at[2], dev_pair
        ),
        remote(
            d_ref.at[:, other_cols], qd.at[own_tan], swap_send.at[3], swap_recv.at[3], dev_pair
        ),
    ]
    swap_in = [
        remote(
            k_ref.at[:, other_cols], kv.at[second, 0:HEAD_DIM],
            swap_send.at[0], swap_recv.at[0], dev_pair,
        ),
        remote(
            v_ref.at[:, other_cols], kv.at[second, HEAD_DIM : 2 * HEAD_DIM],
            swap_send.at[1], swap_recv.at[1], dev_pair,
        ),
        remote(
            q_ref.at[:, other_cols], qd.at[other_rows], swap_send.at[2], swap_recv.at[2], dev_pair
        ),
        remote(
            d_ref.at[:, other_cols], qd.at[other_tan], swap_send.at[3], swap_recv.at[3], dev_pair
        ),
    ]
    for copy in swap:
        copy.start()

    def ring(way, s, o, src_p, dst_p):
        j = part_of(o)
        return remote(
            chunk(src_p, core, j), chunk(dst_p, core, j),
            ring_send.at[way, s - 1, o], ring_recv.at[way, s - 1, o],
            dev_next if way == 0 else dev_prev,
        )

    def sibling(p, o, core_):
        place = chunk(p, core_, part_of(o))
        return remote(place, place, sib_send.at[p, o], sib_recv.at[p, o], dev_sib)

    local[0].wait()
    local[1].wait()
    ring(0, 1, 0, 0, 1).start()
    ring(1, 1, 0, 0, 2).start()
    sibling(0, 0, core).start()

    def w_copy(n, src, dst, device):
        return remote(src, dst, w_send.at[n], w_recv.at[n], device)

    def w_piece(x_hi_, y_, piece):
        return wbuf.at[w_rows(x_hi_, y_, piece)]

    def w_half(x_hi_, y_, part):
        start = (x_hi_ * N_Y + y_) * 256 + core * 128 + part * 64
        return wbuf.at[pl.ds(pl.multiple_of(start, 64), 64)]

    own_w = w_piece(x_hi, y, core)
    across_w = w_piece(1 - x_hi, y, core)
    y_far = lax.rem(y + 2, N_Y)
    w_src = w_ref.at[pl.ds(pl.multiple_of(core * 128, 128), 128), other_half]
    local[5].wait()
    w_copy(0, w_src, own_w, dev_across).start()
    w_copy(1, own_w, own_w, dev_up).start()
    w_copy(2, own_w, own_w, dev_down).start()

    swap_in[0].wait_recv()
    swap_in[1].wait_recv()
    ring(0, 1, 1, 0, 1).start()
    ring(1, 1, 1, 0, 2).start()
    sibling(0, 1, core).start()

    def w_sibling(n, x_hi_, y_, core_):
        place = w_piece(x_hi_, y_, core_)
        return w_copy(n, place, place, dev_sib)

    def w_middle():
        w_copy(0, across_w, across_w, dev_across).wait_recv()
        w_copy(5, across_w, across_w, dev_up).start()
        w_copy(6, across_w, across_w, dev_down).start()
        below, above = w_piece(x_hi, y_prev, core), w_piece(x_hi, y_next, core)
        w_copy(1, below, below, dev_up).wait_recv()
        onward = w_half(x_hi, y_prev, 0)
        w_copy(3, onward, onward, dev_up).start()
        w_copy(2, above, above, dev_down).wait_recv()
        onward = w_half(x_hi, y_next, 1)
        w_copy(4, onward, onward, dev_down).start()
        w_sibling(9, 1 - x_hi, y, core).start()
        w_sibling(10, x_hi, y_prev, core).start()
        w_sibling(11, x_hi, y_next, core).start()

    def w_late():
        below, above = w_piece(1 - x_hi, y_prev, core), w_piece(1 - x_hi, y_next, core)
        w_copy(5, below, below, dev_up).wait_recv()
        onward = w_half(1 - x_hi, y_prev, 0)
        w_copy(7, onward, onward, dev_up).start()
        w_copy(6, above, above, dev_down).wait_recv()
        onward = w_half(1 - x_hi, y_next, 1)
        w_copy(8, onward, onward, dev_down).start()
        w_sibling(13, 1 - x_hi, y_prev, core).start()
        w_sibling(14, 1 - x_hi, y_next, core).start()
        place = w_half(x_hi, y_far, 0)
        w_copy(3, place, place, dev_up).wait_recv()
        place = w_half(x_hi, y_far, 1)
        w_copy(4, place, place, dev_down).wait_recv()
        w_sibling(12, x_hi, y_far, core).start()

    def w_last():
        place = w_half(1 - x_hi, y_far, 0)
        w_copy(7, place, place, dev_up).wait_recv()
        place = w_half(1 - x_hi, y_far, 1)
        w_copy(8, place, place, dev_down).wait_recv()
        w_sibling(15, 1 - x_hi, y_far, core).start()

    def w_finish():
        w_sibling(9, 1 - x_hi, y, 1 - core).wait_recv()
        w_sibling(10, x_hi, y_prev, 1 - core).wait_recv()
        w_sibling(11, x_hi, y_next, 1 - core).wait_recv()
        w_sibling(12, x_hi, y_far, 1 - core).wait_recv()
        w_sibling(13, 1 - x_hi, y_prev, 1 - core).wait_recv()
        w_sibling(14, 1 - x_hi, y_next, 1 - core).wait_recv()
        w_sibling(15, 1 - x_hi, y_far, 1 - core).wait_recv()

    high[...] = jnp.full(high.shape, -1e30, F32)
    acc[...] = jnp.zeros(acc.shape, F32)
    for copy in local[2:5]:
        copy.wait()
    swap_in[2].wait_recv()
    swap_in[3].wait_recv()
    direction = dirb[...].astype(F32)
    squares = jnp.sum((direction * direction).reshape(rows // 8, 8, 2 * HEAD_DIM), axis=0)
    residual_part = squares[:, :HEAD_DIM] + squares[:, HEAD_DIM:]

    def service(h):
        b, o = lax.div(h, 2), lax.rem(h, 2)
        s = b + 1
        back_p, ahead_p = 2 * s - 1, 2 * s

        @pl.when(s < half_z)
        def _():
            ring(0, s, o, back_p, back_p).wait_recv()

            @pl.when(s + 1 < half_z)
            def _():
                ring(0, s + 1, o, back_p, back_p + 2).start()

            @pl.when((s + 1 == half_z) & (o == 0))
            def _():
                ring(0, s + 1, o, back_p, back_p + 2).start()

            ring(1, s, o, ahead_p, ahead_p).wait_recv()

            @pl.when(s + 1 < half_z)
            def _():
                ring(1, s + 1, o, ahead_p, ahead_p + 2).start()

            @pl.when((s + 1 == half_z) & (o == 1))
            def _():
                ring(1, s + 1, o, ahead_p, n_z - 1).start()

            sibling(back_p, o, core).start()
            sibling(ahead_p, o, core).start()

        @pl.when((s == half_z) & (o == 0))
        def _():
            ring(0, s, o, back_p, back_p).wait_recv()
            sibling(back_p, o, core).start()

        @pl.when((s == half_z) & (o == 1))
        def _():
            ring(1, s, o, back_p, back_p).wait_recv()
            sibling(back_p, o, core).start()

    def unit_rows(h):
        start = lax.div(h, 2) * (2 * unit) + part_of(lax.rem(h, 2)) * unit
        return pl.ds(pl.multiple_of(start, 16), unit)

    ones = jnp.ones((unit, HEAD_DIM), BF16)

    def forward(h):
        b, o = lax.div(h, 2), lax.rem(h, 2)

        @pl.when(b == 0)
        def _():
            sibling(0, o, 1 - core).wait_recv()

        sibling(2 * b + 1, o, 1 - core).wait_recv()

        @pl.when(b + 1 < half_z)
        def _():
            sibling(2 * b + 2, o, 1 - core).wait_recv()

        here = unit_rows(h)
        keys = kv[here, 0:HEAD_DIM]
        values = kv[here, HEAD_DIM : 2 * HEAD_DIM]
        scores = dot_nt(qd[0:both], keys)
        tangents = dot_nt(qd[both : 2 * both], keys)
        old = high[...]
        new = jnp.maximum(old, jnp.max(scores, axis=1, keepdims=True))
        high[...] = new
        highs[h] = new
        factor = jnp.exp2((old - new) * EXP2_SCALE)
        weights = jnp.exp2((scores - new) * EXP2_SCALE)
        weighted = weights * tangents
        pw[h, 0:both] = weights.astype(BF16)
        pw[h, both : 2 * both] = weighted.astype(BF16)
        mixed = dot_nn(pw[h], jnp.concatenate([values, ones], axis=1))
        acc[0:both] = acc[0:both] * factor + mixed[0:both]
        acc[both : 2 * both] = acc[both : 2 * both] * factor + mixed[both : 2 * both]

    n_units = n_z
    service(0)

    @pl.loop(1, n_units)
    def _(h):
        service(h)

        @pl.when(h == 5)
        def _():
            w_middle()

        @pl.when(h == 12)
        def _():
            w_late()

        forward(h - 1)

    w_last()
    forward(n_units - 1)

    totals = acc[0:both, HEAD_DIM : 2 * HEAD_DIM]
    attended = acc[0:both, 0:HEAD_DIM] / totals
    att[...] = attended
    tbuf[...] = (
        (acc[both : 2 * both, 0:HEAD_DIM] - acc[both : 2 * both, HEAD_DIM : 2 * HEAD_DIM] * attended)
        * (SCALING / totals)
    ).astype(BF16)

    def window_start(i):
        return lax.div(((both // 16 - 3) * i + 3), n_group - 1) * 16

    def window(i):
        return pl.ds(pl.multiple_of(window_start(i), 16), WINDOW)

    def head_cols(h_):
        return pl.ds(pl.multiple_of(h_ * HEAD_DIM, HEAD_DIM), HEAD_DIM)

    def t_copy(group_, x_lo_, slot):
        return remote(
            tbuf.at[window(group_)], tin.at[:, head_cols(head)],
            t_send.at[slot], t_recv.at[head], (group_, at_ctx(z, x_lo_, core)),
        )

    def t_arrival(h_):
        return remote(
            tbuf.at[window(0)], tin.at[:, head_cols(h_)], t_send.at[0], t_recv.at[h_], dev_pair
        )

    t_copy(group, 1 - x_lo, 0).start()

    @pl.loop(1, n_group)
    def _(i):
        other = lax.rem(group + i, n_group)
        t_copy(other, x_lo, 2 * i).start()
        t_copy(other, 1 - x_lo, 2 * i + 1).start()

    tin[:, head_cols(head)] = tbuf[window(group)]
    w_finish()

    @pl.loop(0, n_heads)
    def _(h_):
        @pl.when(h_ != head)
        def _():
            t_arrival(h_).wait_recv()

    counted = window_start(group + 1) - window_start(group)
    row_id = lax.broadcasted_iota(jnp.int32, (WINDOW, HEAD_DIM), 0)
    curve = jnp.zeros((8, HEAD_DIM), F32)
    step = wide // 3
    for n in range(3):
        cols = slice(n * step, (n + 1) * step)
        proj = dot_nn(tin[...], wbuf[:, cols])
        plow[:, cols] = proj.astype(BF16)
        squared = proj * proj
        lanes = squared[:, 0:HEAD_DIM]
        for m in range(1, step // HEAD_DIM):
            lanes = lanes + squared[:, m * HEAD_DIM : (m + 1) * HEAD_DIM]
        lanes = jnp.where(row_id < counted, lanes, 0.0)
        curve = curve + jnp.sum(lanes.reshape(WINDOW // 8, 8, HEAD_DIM), axis=0)

    def c_copy(h_):
        return remote(
            cout.at[:, head_cols(h_)], cin.at[x_lo, group],
            c_send.at[h_], c_recv.at[x_lo * n_group + group],
            (lax.div(h_, 2), at_ctx(z, lax.rem(h_, 2), core)),
        )

    def c_arrival(x_lo_, group_):
        return remote(
            cout.at[:, head_cols(0)], cin.at[x_lo_, group_],
            c_send.at[0], c_recv.at[x_lo_ * n_group + group_], dev_pair,
        )

    block = 512
    for n in range(n_heads * HEAD_DIM // block):
        at = slice(n * block, (n + 1) * block)
        cout[:, at] = dot_nt(plow[...], wbuf[at]).astype(BF16)

        @pl.loop(n * (block // HEAD_DIM), (n + 1) * (block // HEAD_DIM))
        def _(h_):
            @pl.when(h_ != head)
            def _():
                c_copy(h_).start()

    cin[x_lo, group] = cout[:, head_cols(head)]

    red_z[z, 0:8] = curve
    red_z[z, 8:16] = residual_part

    @pl.loop(1, n_z)
    def _(i):
        other = lax.rem(z + i, n_z)
        remote(
            red_z.at[z], red_z.at[z], red_send.at[i], red_recv.at[z],
            (group, at_ctx(other, x_lo, core)),
        ).start()

    @pl.loop(0, 2 * n_group)
    def _(i):
        x_lo_, group_ = lax.div(i, n_group), lax.rem(i, n_group)

        @pl.when(i != x_lo * n_group + group)
        def _():
            c_arrival(x_lo_, group_).wait_recv()

    starts = [((both // 16 - 3) * i + 3) // (n_group - 1) * 16 for i in range(n_group)]
    for i in range(n_group):
        cbuf[starts[i] : starts[i] + WINDOW] = (
            cin[0, i].astype(F32) + cin[1, i].astype(F32)
        ).astype(BF16)
    centering = jnp.sum(cbuf[...].astype(F32) * att[...], axis=1, keepdims=True)

    qg[...] = jnp.zeros(qg.shape, F32)

    def backward(h):
        here = unit_rows(h)
        keys = kv[here, 0:HEAD_DIM]
        values = kv[here, HEAD_DIM : 2 * HEAD_DIM]
        back = dot_nt(cbuf[...], values)
        grad = (pw[h, 0:both].astype(F32) * (back - centering)).astype(BF16)
        factor = jnp.exp2((highs[h] - high[...]) * EXP2_SCALE)
        qg[...] += dot_nn(grad, keys) * factor

    @pl.loop(0, 6)
    def _(h):
        backward(h)

    def red_arrival(buf, i, base):
        return remote(buf.at[i], buf.at[i], red_send.at[0], red_recv.at[base + i], dev_pair)

    @pl.loop(1, n_z)
    def _(i):
        red_arrival(red_z, lax.rem(z + i, n_z), 0).wait_recv()

    red_g[group] = jnp.sum(red_z[...], axis=0)

    @pl.loop(1, n_group)
    def _(i):
        other = lax.rem(group + i, n_group)
        remote(
            red_g.at[group], red_g.at[group], red_send.at[n_z + i], red_recv.at[n_z + group],
            (other, ctx),
        ).start()

    @pl.loop(6, 11)
    def _(h):
        backward(h)

    @pl.loop(1, n_group)
    def _(i):
        red_arrival(red_g, lax.rem(group + i, n_group), n_z).wait_recv()

    place = 2 * x_lo + core
    red_c[place] = jnp.sum(red_g[...], axis=0)

    @pl.loop(1, 4)
    def _(i):
        other = lax.rem(place + i, 4)
        remote(
            red_c.at[place], red_c.at[place],
            red_send.at[n_z + n_group + i], red_recv.at[n_z + n_group + place],
            (group, 4 * z + other),
        ).start()

    @pl.loop(11, n_units)
    def _(h):
        backward(h)

    scale = SCALING / acc[0:both, HEAD_DIM : 2 * HEAD_DIM]
    qg[...] = qg[...] * scale
    back_copy = remote(
        qg.at[other_rows], qg_in, back_send.at[0], back_recv.at[0], dev_pair
    )
    back_copy.start()

    @pl.loop(1, 4)
    def _(i):
        red_arrival(red_c, lax.rem(place + i, 4), n_z + n_group).wait_recv()

    sums = jnp.sum(red_c[...], axis=0)
    curvature = jnp.sum(jnp.sum(sums[0:8], axis=0, keepdims=True), axis=1, keepdims=True)
    residual_sq = jnp.sum(jnp.sum(sums[8:16], axis=0, keepdims=True), axis=1, keepdims=True)
    step_size = residual_sq / curvature
    out_ref[:, own_cols] = dirb[:, own_cols].astype(F32) - step_size * qg[own_rows]
    back_copy.wait_recv()
    out_ref[:, other_cols] = dirb[:, other_cols].astype(F32) - step_size * qg_in[...]

    back_copy.wait_send()
    for copy in swap:
        copy.wait_send()

    @pl.loop(0, 2 * (half_z - 1))
    def _(i):
        s, o = lax.div(i, 2) + 1, lax.rem(i, 2)
        ring(0, s, o, 1, 1).wait_send()
        ring(1, s, o, 1, 1).wait_send()
        sibling(2 * s - 1, o, core).wait_send()
        sibling(2 * s, o, core).wait_send()

    ring(0, half_z, 0, 1, 1).wait_send()
    ring(1, half_z, 1, 1, 1).wait_send()
    for o in range(2):
        sibling(0, o, core).wait_send()
        sibling(n_z - 1, o, core).wait_send()
    for n in (0, 1, 2, 5, 6):
        w_copy(n, own_w, own_w, dev_up).wait_send()
    for n in (3, 4, 7, 8):
        w_copy(n, w_half(x_hi, y, 0), w_half(x_hi, y, 0), dev_up).wait_send()
    for n in range(9, 16):
        w_sibling(n, x_hi, y, core).wait_send()
    t_copy(group, 1 - x_lo, 0).wait_send()

    @pl.loop(2, n_heads)
    def _(i):
        t_copy(0, 0, i).wait_send()

    @pl.loop(0, n_heads)
    def _(h_):
        @pl.when(h_ != head)
        def _():
            c_copy(h_).wait_send()

    def red_sent(buf, n):
        remote(buf.at[0], buf.at[0], red_send.at[n], red_recv.at[0], dev_pair).wait_send()

    @pl.loop(1, n_z)
    def _(i):
        red_sent(red_z, i)

    @pl.loop(1, n_group)
    def _(i):
        red_sent(red_g, n_z + i)

    @pl.loop(1, 4)
    def _(i):
        red_sent(red_c, n_z + n_group + i)


def body(n_group, n_z, queries, key_rows, value_rows, query_dir, out_weight):
    rows = queries.shape[0]
    both, unit = 2 * rows, 4 * rows
    width = out_weight.shape[1]
    n_heads = 2 * n_group
    any_spec = pl.BlockSpec(memory_space=pl.ANY)
    dma = pltpu.SemaphoreType.DMA
    n_red = n_z + n_group + 4
    return pl.pallas_call(
        functools.partial(kernel, n_group, n_z, rows),
        out_shape=jax.ShapeDtypeStruct((rows, 2 * HEAD_DIM), F32),
        in_specs=[any_spec] * 5,
        out_specs=pl.BlockSpec(memory_space=pltpu.VMEM),
        scratch_shapes=[
            pltpu.VMEM((n_z * unit, 2 * HEAD_DIM), BF16),
            pltpu.VMEM((2 * both, HEAD_DIM), BF16),
            pltpu.VMEM((n_z, 2 * both, unit), BF16),
            pltpu.VMEM((n_z, both, 1), F32),
            pltpu.VMEM((both, 1), F32),
            pltpu.VMEM((2 * both, 2 * HEAD_DIM), F32),
            pltpu.VMEM((rows, 2 * HEAD_DIM), BF16),
            pltpu.VMEM((both, HEAD_DIM), F32),
            pltpu.VMEM((both, HEAD_DIM), BF16),
            pltpu.VMEM((WINDOW, n_heads * HEAD_DIM), BF16),
            pltpu.VMEM((n_heads * HEAD_DIM, width // 2), BF16),
            pltpu.VMEM((WINDOW, width // 2), BF16),
            pltpu.VMEM((WINDOW, n_heads * HEAD_DIM), BF16),
            pltpu.VMEM((2, n_group, WINDOW, HEAD_DIM), BF16),
            pltpu.VMEM((both, HEAD_DIM), BF16),
            pltpu.VMEM((both, HEAD_DIM), F32),
            pltpu.VMEM((rows, HEAD_DIM), F32),
            pltpu.VMEM((n_z, 16, HEAD_DIM), F32),
            pltpu.VMEM((n_group, 16, HEAD_DIM), F32),
            pltpu.VMEM((4, 16, HEAD_DIM), F32),
            dma((6,)),
            dma((4,)), dma((4,)),
            dma((2, n_z // 2, 2)), dma((2, n_z // 2, 2)),
            dma((n_z, 2)), dma((n_z, 2)),
            dma((16,)), dma((16,)),
            dma((n_heads,)), dma((n_heads,)),
            dma((n_heads,)), dma((n_heads,)),
            dma((n_red,)), dma((n_red,)),
            dma((1,)), dma((1,)),
        ],
        compiler_params=pltpu.CompilerParams(
            collective_id=0, has_side_effects=True, vmem_limit_bytes=60 * 1024 * 1024
        ),
        name="gauss_newton_layer",
    )(queries, key_rows, value_rows, query_dir, out_weight)


def solution(mesh):
    n_group, n_ctx = mesh.shape["group"], mesh.shape["ctx"]
    in_specs = (
        P("ctx", "group"),
        P("ctx", "group"),
        P("ctx", "group"),
        P("ctx", "group"),
        P("group", None),
    )
    return jax.shard_map(
        functools.partial(body, n_group, n_ctx // (N_XLO * N_CORE)),
        mesh=mesh, in_specs=in_specs, out_specs=P("ctx", "group"), check_vma=False,
    )
```

```python
import functools
import math

import jax
import jax.numpy as jnp
from jax import lax
from jax.experimental import pallas as pl
from jax.experimental.pallas import tpu as pltpu
from jax.sharding import PartitionSpec as P

MESH = pl.DeviceIdType.MESH
HEAD_DIM = 128
SCALING = HEAD_DIM ** (-0.5)
EXP2_SCALE = SCALING * math.log2(math.e)
N_Y, N_XLO, N_CORE = 4, 2, 2
WINDOW = 48
F32, BF16 = jnp.float32, jnp.bfloat16


def dot_nt(a, b):
    return lax.dot_general(a, b, (((1,), (1,)), ((), ())), preferred_element_type=F32)


def dot_nn(a, b):
    return lax.dot_general(a, b, (((1,), (0,)), ((), ())), preferred_element_type=F32)


def kernel(
    n_group, n_z, rows,
    q_ref, k_ref, v_ref, d_ref, w_ref, out_ref,
    kv, qd, pw, highs, high, acc, dirb, att, tbuf, tin, wbuf, plow, cout, cin, cbuf, qg, qg_in,
    red_z, red_g, red_c,
    local_sem, swap_send, swap_recv, ring_send, ring_recv, sib_send, sib_recv,
    w_send, w_recv, t_send, t_recv, c_send, c_recv, red_send, red_recv, back_send, back_recv,
):
    group, ctx = lax.axis_index("group"), lax.axis_index("ctx")
    x_hi, y = lax.div(group, N_Y), lax.rem(group, N_Y)
    z, x_lo, core = lax.div(ctx, 4), lax.rem(lax.div(ctx, 2), 2), lax.rem(ctx, 2)
    head = 2 * group + x_lo
    both = 2 * rows
    unit = 4 * rows
    half_z = n_z // 2
    n_heads = 2 * n_group
    wide = wbuf.shape[1]

    def at_ctx(z_, x_lo_, core_):
        return 4 * z_ + 2 * x_lo_ + core_

    z_next, z_prev = lax.rem(z + 1, n_z), lax.rem(z + n_z - 1, n_z)
    dev_next = (group, at_ctx(z_next, x_lo, core))
    dev_prev = (group, at_ctx(z_prev, x_lo, core))
    dev_sib = (group, at_ctx(z, x_lo, 1 - core))
    dev_pair = (group, at_ctx(z, 1 - x_lo, core))
    dev_across = ((1 - x_hi) * N_Y + y, at_ctx(z, 1 - x_lo, core))
    y_next, y_prev = lax.rem(y + 1, N_Y), lax.rem(y + N_Y - 1, N_Y)
    dev_up = (x_hi * N_Y + y_next, ctx)
    dev_down = (x_hi * N_Y + y_prev, ctx)

    def remote(src, dst, send, recv, device):
        return pltpu.make_async_remote_copy(
            src_ref=src, dst_ref=dst, send_sem=send, recv_sem=recv,
            device_id=device, device_id_type=MESH,
        )

    def part_of(o):
        return x_lo + o - 2 * x_lo * o

    def chunk_rows(p, core_, j):
        start = lax.div(p, 2) * (2 * unit) + j * unit + lax.rem(p, 2) * both + core_ * rows
        return pl.ds(pl.multiple_of(start, 16), rows)

    def chunk(p, core_, j):
        return kv.at[chunk_rows(p, core_, j)]

    own_cols = pl.ds(pl.multiple_of(x_lo * HEAD_DIM, HEAD_DIM), HEAD_DIM)
    other_cols = pl.ds(pl.multiple_of((1 - x_lo) * HEAD_DIM, HEAD_DIM), HEAD_DIM)
    own_rows = pl.ds(pl.multiple_of(x_lo * rows, 16), rows)
    other_rows = pl.ds(pl.multiple_of((1 - x_lo) * rows, 16), rows)
    own_tan = pl.ds(pl.multiple_of(both + x_lo * rows, 16), rows)
    other_tan = pl.ds(pl.multiple_of(both + (1 - x_lo) * rows, 16), rows)
    first = chunk_rows(0, core, x_lo)
    second = chunk_rows(0, core, 1 - x_lo)
    own_half = pl.ds(pl.multiple_of(x_lo * wide, 128), wide)
    other_half = pl.ds(pl.multiple_of((1 - x_lo) * wide, 128), wide)

    def w_rows(x_hi_, y_, piece):
        start = (x_hi_ * N_Y + y_) * 256 + piece * 128
        return pl.ds(pl.multiple_of(start, 128), 128)

    local = [
        pltpu.make_async_copy(k_ref.at[:, own_cols], kv.at[first, 0:HEAD_DIM], local_sem.at[0]),
        pltpu.make_async_copy(
            v_ref.at[:, own_cols], kv.at[first, HEAD_DIM : 2 * HEAD_DIM], local_sem.at[1]
        ),
        pltpu.make_async_copy(q_ref.at[:, own_cols], qd.at[own_rows], local_sem.at[2]),
        pltpu.make_async_copy(d_ref.at[:, own_cols], qd.at[own_tan], local_sem.at[3]),
        pltpu.make_async_copy(d_ref, dirb, local_sem.at[4]),
        pltpu.make_async_copy(
            w_ref.at[:, own_half],
            wbuf.at[pl.ds(pl.multiple_of(group * 256, 256), 256)],
            local_sem.at[5],
        ),
    ]
    for copy in local:
        copy.start()

    barrier = pltpu.get_barrier_semaphore()

    def greet(device):
        pl.semaphore_signal(barrier, inc=1, device_id=device, device_id_type=MESH)

    greet(dev_next)
    greet(dev_prev)
    greet(dev_sib)
    greet(dev_pair)
    for i in range(1, n_group):
        other = lax.rem(group + i, n_group)
        greet((other, at_ctx(z, x_lo, core)))
        greet((other, at_ctx(z, 1 - x_lo, core)))
    pl.semaphore_wait(barrier, 4 + 2 * (n_group - 1))

    swap = [
        remote(
            k_ref.at[:, other_cols], kv.at[first, 0:HEAD_DIM],
            swap_send.at[0], swap_recv.at[0], dev_pair,
        ),
        remote(
            v_ref.at[:, other_cols], kv.at[first, HEAD_DIM : 2 * HEAD_DIM],
            swap_send.at[1], swap_recv.at[1], dev_pair,
        ),
        remote(
            q_ref.at[:, other_cols], qd.at[own_rows], swap_send.at[2], swap_recv.at[2], dev_pair
        ),
        remote(
            d_ref.at[:, other_cols], qd.at[own_tan], swap_send.at[3], swap_recv.at[3], dev_pair
        ),
    ]
    swap_in = [
        remote(
            k_ref.at[:, other_cols], kv.at[second, 0:HEAD_DIM],
            swap_send.at[0], swap_recv.at[0], dev_pair,
        ),
        remote(
            v_ref.at[:, other_cols], kv.at[second, HEAD_DIM : 2 * HEAD_DIM],
            swap_send.at[1], swap_recv.at[1], dev_pair,
        ),
        remote(
            q_ref.at[:, other_cols], qd.at[other_rows], swap_send.at[2], swap_recv.at[2], dev_pair
        ),
        remote(
            d_ref.at[:, other_cols], qd.at[other_tan], swap_send.at[3], swap_recv.at[3], dev_pair
        ),
    ]
    swap[0].start()
    swap[1].start()

    def ring(way, s, o, f, src_p, dst_p):
        j = part_of(o)
        cols = slice(f * HEAD_DIM, (f + 1) * HEAD_DIM)
        return remote(
            kv.at[chunk_rows(src_p, core, j), cols], kv.at[chunk_rows(dst_p, core, j), cols],
            ring_send.at[way, s - 1, o, f], ring_recv.at[way, s - 1, o, f],
            dev_next if way == 0 else dev_prev,
        )

    def sibling(p, o, core_):
        place = chunk(p, core_, part_of(o))
        return remote(place, place, sib_send.at[p, o], sib_recv.at[p, o], dev_sib)

    local[0].wait()
    local[1].wait()
    for f in range(2):
        ring(0, 1, 0, f, 0, 1).start()
        ring(1, 1, 0, f, 0, 2).start()
    swap[2].start()
    swap[3].start()
    sibling(0, 0, core).start()

    def w_copy(n, src, dst, device):
        return remote(src, dst, w_send.at[n], w_recv.at[n], device)

    def w_piece(x_hi_, y_, piece):
        return wbuf.at[w_rows(x_hi_, y_, piece)]

    def w_half(x_hi_, y_, part):
        start = (x_hi_ * N_Y + y_) * 256 + core * 128 + part * 64
        return wbuf.at[pl.ds(pl.multiple_of(start, 64), 64)]

    own_w = w_piece(x_hi, y, core)
    across_w = w_piece(1 - x_hi, y, core)
    y_far = lax.rem(y + 2, N_Y)
    w_src = w_ref.at[pl.ds(pl.multiple_of(core * 128, 128), 128), other_half]
    local[5].wait()
    w_copy(0, w_src, own_w, dev_across).start()
    w_copy(1, own_w, own_w, dev_up).start()
    w_copy(2, own_w, own_w, dev_down).start()

    for f in range(2):
        swap_in[f].wait_recv()
        ring(0, 1, 1, f, 0, 1).start()
        ring(1, 1, 1, f, 0, 2).start()
    sibling(0, 1, core).start()

    def w_sibling(n, x_hi_, y_, core_):
        place = w_piece(x_hi_, y_, core_)
        return w_copy(n, place, place, dev_sib)

    def w_middle():
        w_copy(0, across_w, across_w, dev_across).wait_recv()
        w_copy(5, across_w, across_w, dev_up).start()
        w_copy(6, across_w, across_w, dev_down).start()
        below, above = w_piece(x_hi, y_prev, core), w_piece(x_hi, y_next, core)
        w_copy(1, below, below, dev_up).wait_recv()
        onward = w_half(x_hi, y_prev, 0)
        w_copy(3, onward, onward, dev_up).start()
        w_copy(2, above, above, dev_down).wait_recv()
        onward = w_half(x_hi, y_next, 1)
        w_copy(4, onward, onward, dev_down).start()
        w_sibling(9, 1 - x_hi, y, core).start()
        w_sibling(10, x_hi, y_prev, core).start()
        w_sibling(11, x_hi, y_next, core).start()

    def w_late():
        below, above = w_piece(1 - x_hi, y_prev, core), w_piece(1 - x_hi, y_next, core)
        w_copy(5, below, below, dev_up).wait_recv()
        onward = w_half(1 - x_hi, y_prev, 0)
        w_copy(7, onward, onward, dev_up).start()
        w_copy(6, above, above, dev_down).wait_recv()
        onward = w_half(1 - x_hi, y_next, 1)
        w_copy(8, onward, onward, dev_down).start()
        w_sibling(13, 1 - x_hi, y_prev, core).start()
        w_sibling(14, 1 - x_hi, y_next, core).start()
        place = w_half(x_hi, y_far, 0)
        w_copy(3, place, place, dev_up).wait_recv()
        place = w_half(x_hi, y_far, 1)
        w_copy(4, place, place, dev_down).wait_recv()
        w_sibling(12, x_hi, y_far, core).start()

    def w_last():
        place = w_half(1 - x_hi, y_far, 0)
        w_copy(7, place, place, dev_up).wait_recv()
        place = w_half(1 - x_hi, y_far, 1)
        w_copy(8, place, place, dev_down).wait_recv()
        w_sibling(15, 1 - x_hi, y_far, core).start()

    def w_finish():
        w_sibling(9, 1 - x_hi, y, 1 - core).wait_recv()
        w_sibling(10, x_hi, y_prev, 1 - core).wait_recv()
        w_sibling(11, x_hi, y_next, 1 - core).wait_recv()
        w_sibling(12, x_hi, y_far, 1 - core).wait_recv()
        w_sibling(13, 1 - x_hi, y_prev, 1 - core).wait_recv()
        w_sibling(14, 1 - x_hi, y_next, 1 - core).wait_recv()
        w_sibling(15, 1 - x_hi, y_far, 1 - core).wait_recv()

    high[...] = jnp.full(high.shape, -1e30, F32)
    acc[...] = jnp.zeros(acc.shape, F32)
    for copy in local[2:5]:
        copy.wait()
    swap_in[2].wait_recv()
    swap_in[3].wait_recv()
    direction = dirb[...].astype(F32)
    squares = jnp.sum((direction * direction).reshape(rows // 8, 8, 2 * HEAD_DIM), axis=0)
    residual_part = squares[:, :HEAD_DIM] + squares[:, HEAD_DIM:]

    def service(h):
        b, o = lax.div(h, 2), lax.rem(h, 2)
        s = b + 1
        back_p, ahead_p = 2 * s - 1, 2 * s

        @pl.when(s + 1 < half_z)
        def _():
            for f in range(2):
                ring(0, s, o, f, back_p, back_p).wait_recv()
                ring(0, s + 1, o, f, back_p, back_p + 2).start()
                ring(1, s, o, f, ahead_p, ahead_p).wait_recv()
                ring(1, s + 1, o, f, ahead_p, ahead_p + 2).start()

        @pl.when(s + 1 == half_z)
        def _():
            for f in range(2):
                ring(0, s, o, f, back_p, back_p).wait_recv()

                @pl.when(o == 0)
                def _():
                    ring(0, s + 1, o, f, back_p, back_p + 2).start()

                ring(1, s, o, f, ahead_p, ahead_p).wait_recv()

                @pl.when(o == 1)
                def _():
                    ring(1, s + 1, o, f, ahead_p, n_z - 1).start()

        @pl.when(s < half_z)
        def _():
            sibling(back_p, o, core).start()
            sibling(ahead_p, o, core).start()

        @pl.when(s == half_z)
        def _():
            for f in range(2):

                @pl.when(o == 0)
                def _():
                    ring(0, s, o, f, back_p, back_p).wait_recv()

                @pl.when(o == 1)
                def _():
                    ring(1, s, o, f, back_p, back_p).wait_recv()

            sibling(back_p, o, core).start()

    def unit_rows(h):
        start = lax.div(h, 2) * (2 * unit) + part_of(lax.rem(h, 2)) * unit
        return pl.ds(pl.multiple_of(start, 16), unit)

    ones = jnp.ones((unit, HEAD_DIM), BF16)

    def forward(h):
        b, o = lax.div(h, 2), lax.rem(h, 2)

        @pl.when(b == 0)
        def _():
            sibling(0, o, 1 - core).wait_recv()

        sibling(2 * b + 1, o, 1 - core).wait_recv()

        @pl.when(b + 1 < half_z)
        def _():
            sibling(2 * b + 2, o, 1 - core).wait_recv()

        here = unit_rows(h)
        keys = kv[here, 0:HEAD_DIM]
        values = kv[here, HEAD_DIM : 2 * HEAD_DIM]
        scores = dot_nt(qd[0:both], keys)
        tangents = dot_nt(qd[both : 2 * both], keys)
        old = high[...]
        new = jnp.maximum(old, jnp.max(scores, axis=1, keepdims=True))
        high[...] = new
        highs[h] = new
        factor = jnp.exp2((old - new) * EXP2_SCALE)
        weights = jnp.exp2((scores - new) * EXP2_SCALE)
        weighted = weights * tangents
        pw[h, 0:both] = weights.astype(BF16)
        pw[h, both : 2 * both] = weighted.astype(BF16)
        mixed = dot_nn(pw[h], jnp.concatenate([values, ones], axis=1))
        acc[0:both] = acc[0:both] * factor + mixed[0:both]
        acc[both : 2 * both] = acc[both : 2 * both] * factor + mixed[both : 2 * both]

    n_units = n_z
    service(0)

    @pl.loop(1, n_units)
    def _(h):
        service(h)

        @pl.when(h == 5)
        def _():
            w_middle()

        @pl.when(h == 12)
        def _():
            w_late()

        forward(h - 1)

    w_last()
    forward(n_units - 1)

    totals = acc[0:both, HEAD_DIM : 2 * HEAD_DIM]
    attended = acc[0:both, 0:HEAD_DIM] / totals
    att[...] = attended
    tbuf[...] = (
        (acc[both : 2 * both, 0:HEAD_DIM] - acc[both : 2 * both, HEAD_DIM : 2 * HEAD_DIM] * attended)
        * (SCALING / totals)
    ).astype(BF16)

    def window_start(i):
        return lax.div(((both // 16 - 3) * i + 3), n_group - 1) * 16

    def window(i):
        return pl.ds(pl.multiple_of(window_start(i), 16), WINDOW)

    def head_cols(h_):
        return pl.ds(pl.multiple_of(h_ * HEAD_DIM, HEAD_DIM), HEAD_DIM)

    def t_copy(group_, x_lo_, slot):
        return remote(
            tbuf.at[window(group_)], tin.at[:, head_cols(head)],
            t_send.at[slot], t_recv.at[head], (group_, at_ctx(z, x_lo_, core)),
        )

    def t_arrival(h_):
        return remote(
            tbuf.at[window(0)], tin.at[:, head_cols(h_)], t_send.at[0], t_recv.at[h_], dev_pair
        )

    t_copy(group, 1 - x_lo, 0).start()
    for i in range(1, n_group):
        other = lax.rem(group + i, n_group)
        t_copy(other, x_lo, 2 * i).start()
        t_copy(other, 1 - x_lo, 2 * i + 1).start()

    tin[:, head_cols(head)] = tbuf[window(group)]
    w_finish()

    for copy in swap:
        copy.wait_send()

    @pl.loop(0, 2 * (half_z - 1))
    def _(i):
        s, o = lax.div(i, 2) + 1, lax.rem(i, 2)
        for f in range(2):
            ring(0, s, o, f, 1, 1).wait_send()
            ring(1, s, o, f, 1, 1).wait_send()
        sibling(2 * s - 1, o, core).wait_send()
        sibling(2 * s, o, core).wait_send()

    for f in range(2):
        ring(0, half_z, 0, f, 1, 1).wait_send()
        ring(1, half_z, 1, f, 1, 1).wait_send()
    for o in range(2):
        sibling(0, o, core).wait_send()
        sibling(n_z - 1, o, core).wait_send()
    for n in (0, 1, 2, 5, 6):
        w_copy(n, own_w, own_w, dev_up).wait_send()
    for n in (3, 4, 7, 8):
        w_copy(n, w_half(x_hi, y, 0), w_half(x_hi, y, 0), dev_up).wait_send()
    for n in range(9, 16):
        w_sibling(n, x_hi, y, core).wait_send()

    for i in range(1, n_heads):
        t_arrival(lax.rem(head + i, n_heads)).wait_recv()

    counted = window_start(group + 1) - window_start(group)
    row_id = lax.broadcasted_iota(jnp.int32, (WINDOW, HEAD_DIM), 0)
    curve = jnp.zeros((8, HEAD_DIM), F32)
    step = wide // 3
    for n in range(3):
        cols = slice(n * step, (n + 1) * step)
        proj = dot_nn(tin[...], wbuf[:, cols])
        plow[:, cols] = proj.astype(BF16)
        squared = proj * proj
        lanes = squared[:, 0:HEAD_DIM]
        for m in range(1, step // HEAD_DIM):
            lanes = lanes + squared[:, m * HEAD_DIM : (m + 1) * HEAD_DIM]
        lanes = jnp.where(row_id < counted, lanes, 0.0)
        curve = curve + jnp.sum(lanes.reshape(WINDOW // 8, 8, HEAD_DIM), axis=0)

    red_z[z, 0:8] = curve
    red_z[z, 8:16] = residual_part

    def red_copy(buf, here, n, base, device):
        return remote(buf.at[here], buf.at[here], red_send.at[n], red_recv.at[base + here], device)

    def red_arrival(buf, there, base):
        return remote(buf.at[there], buf.at[there], red_send.at[0], red_recv.at[base + there], dev_pair)

    for i in range(1, n_z):
        other = lax.rem(z + i, n_z)
        red_copy(red_z, z, i, 0, (group, at_ctx(other, x_lo, core))).start()

    def c_copy(h_):
        return remote(
            cout.at[:, head_cols(h_)], cin.at[x_lo, group],
            c_send.at[h_], c_recv.at[x_lo * n_group + group],
            (h_ // 2, at_ctx(z, h_ % 2, core)),
        )

    def c_arrival(x_lo_, group_):
        return remote(
            cout.at[:, head_cols(0)], cin.at[x_lo_, group_],
            c_send.at[0], c_recv.at[x_lo_ * n_group + group_], dev_pair,
        )

    block = 512
    for n in range(n_heads * HEAD_DIM // block):
        at = slice(n * block, (n + 1) * block)
        cout[:, at] = dot_nt(plow[...], wbuf[at]).astype(BF16)

        for h_ in range(n * (block // HEAD_DIM), (n + 1) * (block // HEAD_DIM)):

            @pl.when(h_ != head)
            def _():
                c_copy(h_).start()

    cin[x_lo, group] = cout[:, head_cols(head)]

    t_copy(group, 1 - x_lo, 0).wait_send()
    for i in range(2, n_heads):
        t_copy(0, 0, i).wait_send()

    for i in range(1, n_group):
        c_arrival(x_lo, lax.rem(group + i, n_group)).wait_recv()
    for i in range(n_group):
        c_arrival(1 - x_lo, i).wait_recv()

    starts = [((both // 16 - 3) * i + 3) // (n_group - 1) * 16 for i in range(n_group)]
    for i in range(n_group):
        cbuf[starts[i] : starts[i] + WINDOW] = (
            cin[0, i].astype(F32) + cin[1, i].astype(F32)
        ).astype(BF16)
    centering = jnp.sum(cbuf[...].astype(F32) * att[...], axis=1, keepdims=True)

    qg[...] = jnp.zeros(qg.shape, F32)

    def backward(h):
        here = unit_rows(h)
        keys = kv[here, 0:HEAD_DIM]
        values = kv[here, HEAD_DIM : 2 * HEAD_DIM]
        back = dot_nt(cbuf[...], values)
        grad = (pw[h, 0:both].astype(F32) * (back - centering)).astype(BF16)
        factor = jnp.exp2((highs[h] - high[...]) * EXP2_SCALE)
        qg[...] += dot_nn(grad, keys) * factor

    @pl.loop(0, 6)
    def _(h):
        backward(h)

    for i in range(1, n_z):
        red_arrival(red_z, lax.rem(z + i, n_z), 0).wait_recv()
    red_g[head] = jnp.sum(red_z[...], axis=0)
    for i in range(1, n_heads):
        other = lax.rem(head + i, n_heads)
        device = (lax.div(other, 2), at_ctx(z, lax.rem(other, 2), core))
        red_copy(red_g, head, n_z + i, n_z, device).start()

    @pl.loop(6, n_units)
    def _(h):
        backward(h)

    scale = SCALING / acc[0:both, HEAD_DIM : 2 * HEAD_DIM]
    qg[...] = qg[...] * scale
    back_copy = remote(
        qg.at[other_rows], qg_in, back_send.at[0], back_recv.at[0], dev_pair
    )
    back_copy.start()

    for i in range(1, n_heads):
        red_arrival(red_g, lax.rem(head + i, n_heads), n_z).wait_recv()
    red_c[core] = jnp.sum(red_g[...], axis=0)
    last = red_copy(red_c, core, n_z + n_heads, n_z + n_heads, dev_sib)
    last.start()
    for i in range(1, n_z):
        red_copy(red_z, z, i, 0, dev_next).wait_send()
    for i in range(1, n_heads):
        red_copy(red_g, head, n_z + i, n_z, dev_pair).wait_send()
    for h_ in range(n_heads):

        @pl.when(h_ != head)
        def _():
            c_copy(h_).wait_send()

    red_arrival(red_c, 1 - core, n_z + n_heads).wait_recv()
    last.wait_send()
    sums = jnp.sum(red_c[...], axis=0)
    curvature = jnp.sum(jnp.sum(sums[0:8], axis=0, keepdims=True), axis=1, keepdims=True)
    residual_sq = jnp.sum(jnp.sum(sums[8:16], axis=0, keepdims=True), axis=1, keepdims=True)
    step_size = residual_sq / curvature
    out_ref[:, own_cols] = dirb[:, own_cols].astype(F32) - step_size * qg[own_rows]
    back_copy.wait_recv()
    out_ref[:, other_cols] = dirb[:, other_cols].astype(F32) - step_size * qg_in[...]
    back_copy.wait_send()


def body(n_group, n_z, queries, key_rows, value_rows, query_dir, out_weight):
    rows = queries.shape[0]
    both, unit = 2 * rows, 4 * rows
    width = out_weight.shape[1]
    n_heads = 2 * n_group
    any_spec = pl.BlockSpec(memory_space=pl.ANY)
    dma = pltpu.SemaphoreType.DMA
    n_red = n_z + n_heads + 2
    return pl.pallas_call(
        functools.partial(kernel, n_group, n_z, rows),
        out_shape=jax.ShapeDtypeStruct((rows, 2 * HEAD_DIM), F32),
        in_specs=[any_spec] * 5,
        out_specs=pl.BlockSpec(memory_space=pltpu.VMEM),
        scratch_shapes=[
            pltpu.VMEM((n_z * unit, 2 * HEAD_DIM), BF16),
            pltpu.VMEM((2 * both, HEAD_DIM), BF16),
            pltpu.VMEM((n_z, 2 * both, unit), BF16),
            pltpu.VMEM((n_z, both, 1), F32),
            pltpu.VMEM((both, 1), F32),
            pltpu.VMEM((2 * both, 2 * HEAD_DIM), F32),
            pltpu.VMEM((rows, 2 * HEAD_DIM), BF16),
            pltpu.VMEM((both, HEAD_DIM), F32),
            pltpu.VMEM((both, HEAD_DIM), BF16),
            pltpu.VMEM((WINDOW, n_heads * HEAD_DIM), BF16),
            pltpu.VMEM((n_heads * HEAD_DIM, width // 2), BF16),
            pltpu.VMEM((WINDOW, width // 2), BF16),
            pltpu.VMEM((WINDOW, n_heads * HEAD_DIM), BF16),
            pltpu.VMEM((2, n_group, WINDOW, HEAD_DIM), BF16),
            pltpu.VMEM((both, HEAD_DIM), BF16),
            pltpu.VMEM((both, HEAD_DIM), F32),
            pltpu.VMEM((rows, HEAD_DIM), F32),
            pltpu.VMEM((n_z, 16, HEAD_DIM), F32),
            pltpu.VMEM((n_heads, 16, HEAD_DIM), F32),
            pltpu.VMEM((2, 16, HEAD_DIM), F32),
            dma((6,)),
            dma((4,)), dma((4,)),
            dma((2, n_z // 2, 2, 2)), dma((2, n_z // 2, 2, 2)),
            dma((n_z, 2)), dma((n_z, 2)),
            dma((16,)), dma((16,)),
            dma((n_heads,)), dma((n_heads,)),
            dma((n_heads,)), dma((n_heads,)),
            dma((n_red,)), dma((n_red,)),
            dma((1,)), dma((1,)),
        ],
        compiler_params=pltpu.CompilerParams(
            collective_id=0, has_side_effects=True, vmem_limit_bytes=60 * 1024 * 1024
        ),
        name="gauss_newton_layer",
    )(queries, key_rows, value_rows, query_dir, out_weight)


def solution(mesh):
    n_group, n_ctx = mesh.shape["group"], mesh.shape["ctx"]
    in_specs = (
        P("ctx", "group"),
        P("ctx", "group"),
        P("ctx", "group"),
        P("ctx", "group"),
        P("group", None),
    )
    return jax.shard_map(
        functools.partial(body, n_group, n_ctx // (N_XLO * N_CORE)),
        mesh=mesh, in_specs=in_specs, out_specs=P("ctx", "group"), check_vma=False,
    )
```

```python
import functools
import math

import jax
import jax.numpy as jnp
from jax import lax
from jax.experimental import pallas as pl
from jax.experimental.pallas import tpu as pltpu
from jax.sharding import PartitionSpec as P

MESH = pl.DeviceIdType.MESH
HEAD_DIM = 128
SCALING = HEAD_DIM ** (-0.5)
EXP2_SCALE = SCALING * math.log2(math.e)
N_Y, N_XLO, N_CORE = 4, 2, 2
WINDOW = 48
F32, BF16 = jnp.float32, jnp.bfloat16


def dot_nt(a, b):
    return lax.dot_general(a, b, (((1,), (1,)), ((), ())), preferred_element_type=F32)


def dot_nn(a, b):
    return lax.dot_general(a, b, (((1,), (0,)), ((), ())), preferred_element_type=F32)


def kernel(
    n_group, n_z, rows,
    q_ref, k_ref, v_ref, d_ref, w_ref, out_ref,
    kb, vb, qd, pw, highs, high, acc, dirb, att, tbuf, tin, wbuf, plow, cout, cin, cbuf, qg, qg_in,
    red_z, red_g, red_c,
    local_sem, swap_send, swap_recv, ring_send, ring_recv, sib_send, sib_recv,
    w_send, w_recv, t_send, t_recv, c_send, c_recv, red_send, red_recv, back_send, back_recv,
):
    group, ctx = lax.axis_index("group"), lax.axis_index("ctx")
    x_hi, y = lax.div(group, N_Y), lax.rem(group, N_Y)
    z, x_lo, core = lax.div(ctx, 4), lax.rem(lax.div(ctx, 2), 2), lax.rem(ctx, 2)
    head = 2 * group + x_lo
    both = 2 * rows
    unit = 4 * rows
    half_z = n_z // 2
    n_heads = 2 * n_group
    wide = wbuf.shape[1]

    def at_ctx(z_, x_lo_, core_):
        return 4 * z_ + 2 * x_lo_ + core_

    z_next, z_prev = lax.rem(z + 1, n_z), lax.rem(z + n_z - 1, n_z)
    dev_next = (group, at_ctx(z_next, x_lo, core))
    dev_prev = (group, at_ctx(z_prev, x_lo, core))
    dev_sib = (group, at_ctx(z, x_lo, 1 - core))
    dev_pair = (group, at_ctx(z, 1 - x_lo, core))
    dev_across = ((1 - x_hi) * N_Y + y, at_ctx(z, 1 - x_lo, core))
    y_next, y_prev = lax.rem(y + 1, N_Y), lax.rem(y + N_Y - 1, N_Y)
    dev_up = (x_hi * N_Y + y_next, ctx)
    dev_down = (x_hi * N_Y + y_prev, ctx)

    def remote(src, dst, send, recv, device):
        return pltpu.make_async_remote_copy(
            src_ref=src, dst_ref=dst, send_sem=send, recv_sem=recv,
            device_id=device, device_id_type=MESH,
        )

    def own_plane_rows(j):
        return pl.ds(pl.multiple_of(core * both + j * rows, 16), rows)

    own_cols = pl.ds(pl.multiple_of(x_lo * HEAD_DIM, HEAD_DIM), HEAD_DIM)
    other_cols = pl.ds(pl.multiple_of((1 - x_lo) * HEAD_DIM, HEAD_DIM), HEAD_DIM)
    own_rows = pl.ds(pl.multiple_of(x_lo * rows, 16), rows)
    other_rows = pl.ds(pl.multiple_of((1 - x_lo) * rows, 16), rows)
    own_tan = pl.ds(pl.multiple_of(both + x_lo * rows, 16), rows)
    other_tan = pl.ds(pl.multiple_of(both + (1 - x_lo) * rows, 16), rows)
    first = own_plane_rows(x_lo)
    second = own_plane_rows(1 - x_lo)
    own_half = pl.ds(pl.multiple_of(x_lo * wide, 128), wide)
    other_half = pl.ds(pl.multiple_of((1 - x_lo) * wide, 128), wide)

    def w_rows(x_hi_, y_, piece):
        start = (x_hi_ * N_Y + y_) * 256 + piece * 128
        return pl.ds(pl.multiple_of(start, 128), 128)

    local = [
        pltpu.make_async_copy(k_ref.at[:, own_cols], kb.at[first], local_sem.at[0]),
        pltpu.make_async_copy(
            v_ref.at[:, own_cols], vb.at[first], local_sem.at[1]
        ),
        pltpu.make_async_copy(q_ref.at[:, own_cols], qd.at[own_rows], local_sem.at[2]),
        pltpu.make_async_copy(d_ref.at[:, own_cols], qd.at[own_tan], local_sem.at[3]),
        pltpu.make_async_copy(d_ref, dirb, local_sem.at[4]),
        pltpu.make_async_copy(
            w_ref.at[:, own_half],
            wbuf.at[pl.ds(pl.multiple_of(group * 256, 256), 256)],
            local_sem.at[5],
        ),
    ]
    for copy in local:
        copy.start()

    barrier = pltpu.get_barrier_semaphore()

    def greet(device):
        pl.semaphore_signal(barrier, inc=1, device_id=device, device_id_type=MESH)

    greet(dev_next)
    greet(dev_prev)
    greet(dev_sib)
    greet(dev_pair)
    for i in range(1, n_group):
        other = lax.rem(group + i, n_group)
        greet((other, at_ctx(z, x_lo, core)))
        greet((other, at_ctx(z, 1 - x_lo, core)))
    high[...] = jnp.full(high.shape, -1e30, F32)
    acc[...] = jnp.zeros(acc.shape, F32)
    qg[...] = jnp.zeros(qg.shape, F32)
    pl.semaphore_wait(barrier, 4 + 2 * (n_group - 1))

    swap = [
        remote(
            k_ref.at[:, other_cols], kb.at[first],
            swap_send.at[0], swap_recv.at[0], dev_pair,
        ),
        remote(
            v_ref.at[:, other_cols], vb.at[first],
            swap_send.at[1], swap_recv.at[1], dev_pair,
        ),
        remote(
            q_ref.at[:, other_cols], qd.at[own_rows], swap_send.at[2], swap_recv.at[2], dev_pair
        ),
        remote(
            d_ref.at[:, other_cols], qd.at[own_tan], swap_send.at[3], swap_recv.at[3], dev_pair
        ),
    ]
    swap_in = [
        remote(
            k_ref.at[:, other_cols], kb.at[second],
            swap_send.at[0], swap_recv.at[0], dev_pair,
        ),
        remote(
            v_ref.at[:, other_cols], vb.at[second],
            swap_send.at[1], swap_recv.at[1], dev_pair,
        ),
        remote(
            q_ref.at[:, other_cols], qd.at[other_rows], swap_send.at[2], swap_recv.at[2], dev_pair
        ),
        remote(
            d_ref.at[:, other_cols], qd.at[other_tan], swap_send.at[3], swap_recv.at[3], dev_pair
        ),
    ]
    swap[0].start()
    swap[1].start()

    part_start, part_step = x_lo * rows, (1 - 2 * x_lo) * rows
    mine = core * both
    theirs = (1 - core) * both

    def rows_at(way, s, o, offset):
        base = s * (2 * unit) + part_start + o * part_step + offset
        if way == 0:
            base = base - unit
        return pl.ds(pl.multiple_of(base, 16), rows)

    def ring(way, s, o, f, src, dst):
        buf = (kb, vb)[f]
        n = s * 8 + (way * 4 + o * 2 + f)
        return remote(
            buf.at[src], buf.at[dst], ring_send.at[n], ring_recv.at[n],
            dev_next if way == 0 else dev_prev,
        )

    def ring_start(way, s, o, f):
        src = rows_at(1, s - 1, o, mine) if way else rows_at(0, s - 1, o, mine)
        ring(way, s, o, f, src, rows_at(way, s, o, mine)).start()

    def ring_first(way, o, f):
        if o == 0:
            n = 8 + way * 4 + f
            remote(
                (k_ref, v_ref)[f].at[:, own_cols], (kb, vb)[f].at[rows_at(way, 1, 0, mine)],
                ring_send.at[n], ring_recv.at[n], dev_next if way == 0 else dev_prev,
            ).start()
        else:
            ring(way, 1, o, f, rows_at(1, 0, o, mine), rows_at(way, 1, o, mine)).start()

    def ring_wait(way, s, o, f):
        place = rows_at(way, s, o, mine)
        ring(way, s, o, f, place, place).wait_recv()

    def last_start(way, f):
        src = rows_at(way, half_z - 1, way, mine)
        ring(way, half_z, way, f, src, rows_at(0, half_z, way, mine)).start()

    def last_wait(way, f):
        place = rows_at(0, half_z, way, mine)
        ring(way, half_z, way, f, place, place).wait_recv()

    def sibling(p, f, offset):
        place = (kb, vb)[f].at[pl.ds(pl.multiple_of(p * unit + offset, 16), both)]
        return remote(place, place, sib_send.at[p * 2 + f], sib_recv.at[p * 2 + f], dev_sib)

    def sibling_part(p, o, f, offset):
        start = p * unit + part_start + o * part_step + offset
        place = (kb, vb)[f].at[pl.ds(pl.multiple_of(start, 16), rows)]
        n = 2 * n_z + (o * 2 + f if p else 4 + o * 2 + f)
        return remote(place, place, sib_send.at[n], sib_recv.at[n], dev_sib)

    for f in range(2):
        ring_first(0, 0, f)
        ring_first(1, 0, f)
    swap[2].start()
    swap[3].start()
    for f in range(2):
        local[f].wait()
        sibling_part(0, 0, f, mine).start()

    def w_copy(n, src, dst, device):
        return remote(src, dst, w_send.at[n], w_recv.at[n], device)

    def w_piece(x_hi_, y_, piece):
        return wbuf.at[w_rows(x_hi_, y_, piece)]

    def w_half(x_hi_, y_, part):
        start = (x_hi_ * N_Y + y_) * 256 + core * 128 + part * 64
        return wbuf.at[pl.ds(pl.multiple_of(start, 64), 64)]

    y_far = lax.rem(y + 2, N_Y)
    def w_src(q):
        return w_ref.at[pl.ds(pl.multiple_of(core * 128 + q * 64, 64), 64), other_half]

    def w_own(q):
        return w_ref.at[pl.ds(pl.multiple_of(core * 128 + q * 64, 64), 64), own_half]

    for q in range(2):
        w_copy(q, w_src(q), w_half(x_hi, y, q), dev_across).start()
        w_copy(2 + q, w_own(q), w_half(x_hi, y, q), dev_up).start()
        w_copy(4 + q, w_own(1 - q), w_half(x_hi, y, 1 - q), dev_down).start()

    for f in range(2):
        swap_in[f].wait_recv()
        ring_first(0, 1, f)
        ring_first(1, 1, f)
    for f in range(2):
        sibling_part(0, 1, f, mine).start()

    def w_sibling(n, x_hi_, y_, core_):
        place = w_piece(x_hi_, y_, core_)
        return w_copy(n, place, place, dev_sib)

    def w_take(n, x_hi_, y_, part):
        place = w_half(x_hi_, y_, part)
        w_copy(n, place, place, dev_up).wait_recv()

    def w_give(n, x_hi_, y_, part, device):
        place = w_half(x_hi_, y_, part)
        w_copy(n, place, place, device).start()

    x_not = 1 - x_hi

    def w_first():
        w_take(0, x_not, y, 0)
        w_give(8, x_not, y, 0, dev_up)
        w_take(2, x_hi, y_prev, 0)
        w_give(6, x_hi, y_prev, 0, dev_up)
        w_take(4, x_hi, y_next, 1)
        w_give(7, x_hi, y_next, 1, dev_down)

    def w_second():
        w_take(1, x_not, y, 1)
        w_give(10, x_not, y, 1, dev_down)
        w_give(9, x_not, y, 1, dev_up)
        w_give(11, x_not, y, 0, dev_down)
        w_sibling(14, x_not, y, core).start()
        w_take(3, x_hi, y_prev, 1)
        w_sibling(15, x_hi, y_prev, core).start()
        w_take(5, x_hi, y_next, 0)
        w_sibling(16, x_hi, y_next, core).start()

    def w_third():
        w_take(8, x_not, y_prev, 0)
        w_give(12, x_not, y_prev, 0, dev_up)
        w_take(10, x_not, y_next, 1)
        w_give(13, x_not, y_next, 1, dev_down)
        w_take(6, x_hi, y_far, 0)
        w_take(7, x_hi, y_far, 1)
        w_sibling(17, x_hi, y_far, core).start()

    def w_fourth():
        w_take(9, x_not, y_prev, 1)
        w_sibling(18, x_not, y_prev, core).start()
        w_take(11, x_not, y_next, 0)
        w_sibling(19, x_not, y_next, core).start()
        w_take(12, x_not, y_far, 0)
        w_take(13, x_not, y_far, 1)
        w_sibling(20, x_not, y_far, core).start()

    def w_finish():
        local[5].wait()
        w_sibling(14, x_not, y, 1 - core).wait_recv()
        w_sibling(15, x_hi, y_prev, 1 - core).wait_recv()
        w_sibling(16, x_hi, y_next, 1 - core).wait_recv()
        w_sibling(17, x_hi, y_far, 1 - core).wait_recv()
        w_sibling(18, x_not, y_prev, 1 - core).wait_recv()
        w_sibling(19, x_not, y_next, 1 - core).wait_recv()
        w_sibling(20, x_not, y_far, 1 - core).wait_recv()

    def when(condition):
        if isinstance(condition, bool):
            return lambda run: run() if condition else None
        return pl.when(condition)

    def service(s, o):
        def ways(final):
            for f in range(2):
                for way in range(2):
                    ring_wait(way, s, o, f)
                    if final:

                        @when(o == way)
                        def _():
                            last_start(way, f)

                    else:
                        ring_start(way, s + 1, o, f)

            @when(o == 1)
            def _():
                for way in range(2):
                    for f in range(2):
                        sibling(2 * s - 1 + way, f, mine).start()

        @when(s < half_z - 1)
        def _():
            ways(False)

        @when(s == half_z - 1)
        def _():
            ways(True)

        @when(s == half_z)
        def _():
            for f in range(2):
                for way in range(2):

                    @when(o == way)
                    def _():
                        last_wait(way, f)
                        sibling_part(n_z - 1, way, f, mine).start()

    def unit_rows(h):
        return pl.ds(pl.multiple_of(h * unit, 16), unit)

    ones = jnp.ones((unit, HEAD_DIM), BF16)

    def forward(units):
        blocks = []
        for h in units:
            keys = kb[unit_rows(h)]
            blocks.append((dot_nt(qd[0:both], keys), dot_nt(qd[both : 2 * both], keys)))
        old = high[...]
        new = old
        for scores, _ in blocks:
            new = jnp.maximum(new, jnp.max(scores, axis=1, keepdims=True))
        high[...] = new
        factor = jnp.exp2((old - new) * EXP2_SCALE)
        mixed = tangent_mixed = None
        for h, (scores, tangents) in zip(units, blocks):
            weights = jnp.exp2((scores - new) * EXP2_SCALE)
            weighted = (weights * tangents).astype(BF16)
            weights = weights.astype(BF16)
            highs[h] = new
            pw[h] = weights
            values = jnp.concatenate([vb[unit_rows(h)], ones], axis=1)
            a, b = dot_nn(weights, values), dot_nn(weighted, values)
            mixed = a if mixed is None else mixed + a
            tangent_mixed = b if tangent_mixed is None else tangent_mixed + b
        acc[0:both] = acc[0:both] * factor + mixed
        acc[both : 2 * both] = acc[both : 2 * both] * factor + tangent_mixed

    n_units = n_z
    service(1, 0)
    for copy in local[2:5]:
        copy.wait()
    swap_in[2].wait_recv()
    swap_in[3].wait_recv()
    direction = dirb[...].astype(F32)
    squares = jnp.sum((direction * direction).reshape(rows // 8, 8, 2 * HEAD_DIM), axis=0)
    residual_part = squares[:, :HEAD_DIM] + squares[:, HEAD_DIM:]
    for o in range(2):
        for f in range(2):
            sibling_part(0, o, f, theirs).wait_recv()

    service(1, 1)

    @pl.loop(2, half_z + 2)
    def _(s):
        @pl.when(s <= half_z)
        def _():
            service(s, 0)

        @pl.when(s > 2)
        def _():
            for f in range(2):
                sibling(2 * s - 4, f, theirs).wait_recv()

        @pl.when(s <= half_z)
        def _():
            for f in range(2):
                sibling(2 * s - 3, f, theirs).wait_recv()

        @pl.when(s > half_z)
        def _():
            for o in range(2):
                for f in range(2):
                    sibling_part(n_z - 1, o, f, theirs).wait_recv()

        forward([2 * s - 4, 2 * s - 3])

        @pl.when(s == 3)
        def _():
            w_first()

        @pl.when(s == 4)
        def _():
            w_second()

        @pl.when(s == 6)
        def _():
            w_third()

        @pl.when(s == half_z)
        def _():
            w_fourth()

        @pl.when(s <= half_z)
        def _():
            service(s, 1)

    totals = acc[0:both, HEAD_DIM : 2 * HEAD_DIM]
    attended = acc[0:both, 0:HEAD_DIM] / totals
    tbuf[...] = (
        (acc[both : 2 * both, 0:HEAD_DIM] - acc[both : 2 * both, HEAD_DIM : 2 * HEAD_DIM] * attended)
        * (SCALING / totals)
    ).astype(BF16)

    def window_start(i):
        return lax.div(((both // 16 - 3) * i + 3), n_group - 1) * 16

    def window(i):
        return pl.ds(pl.multiple_of(window_start(i), 16), WINDOW)

    def head_cols(h_):
        return pl.ds(pl.multiple_of(h_ * HEAD_DIM, HEAD_DIM), HEAD_DIM)

    def t_copy(group_, x_lo_, slot):
        return remote(
            tbuf.at[window(group_)], tin.at[:, head_cols(head)],
            t_send.at[slot], t_recv.at[head], (group_, at_ctx(z, x_lo_, core)),
        )

    def t_arrival(h_):
        return remote(
            tbuf.at[window(0)], tin.at[:, head_cols(h_)], t_send.at[0], t_recv.at[h_], dev_pair
        )

    t_copy(group, 1 - x_lo, 0).start()
    for i in range(1, n_group):
        other = lax.rem(group + i, n_group)
        t_copy(other, x_lo, 2 * i).start()
        t_copy(other, 1 - x_lo, 2 * i + 1).start()

    tin[:, head_cols(head)] = tbuf[window(group)]
    att[...] = attended
    w_finish()

    for copy in swap:
        copy.wait_send()

    def left(size, sem):
        remote(kb.at[0:size], kb.at[0:size], sem, ring_recv.at[0], dev_next).wait_send()

    for s in range(1, half_z):
        for n in range(8):
            left(rows, ring_send.at[s * 8 + n])
    for way in range(2):
        for f in range(2):
            left(rows, ring_send.at[half_z * 8 + way * 6 + f])
            left(rows, sib_send.at[2 * n_z + way * 2 + f])
            left(rows, sib_send.at[2 * n_z + 4 + way * 2 + f])
    for n in range(2, 2 * n_z - 2):
        left(both, sib_send.at[n])
    for n in range(14):
        w_copy(n, w_half(x_hi, y, 0), w_half(x_hi, y, 0), dev_up).wait_send()
    for n in range(14, 21):
        w_sibling(n, x_hi, y, core).wait_send()

    for i in range(1, n_heads):
        t_arrival(lax.rem(head + i, n_heads)).wait_recv()

    counted = window_start(group + 1) - window_start(group)
    row_id = lax.broadcasted_iota(jnp.int32, (WINDOW, HEAD_DIM), 0)
    curve = jnp.zeros((8, HEAD_DIM), F32)
    step = wide // 3
    for n in range(3):
        cols = slice(n * step, (n + 1) * step)
        proj = dot_nn(tin[...], wbuf[:, cols])
        plow[:, cols] = proj.astype(BF16)
        squared = proj * proj
        lanes = squared[:, 0:HEAD_DIM]
        for m in range(1, step // HEAD_DIM):
            lanes = lanes + squared[:, m * HEAD_DIM : (m + 1) * HEAD_DIM]
        lanes = jnp.where(row_id < counted, lanes, 0.0)
        curve = curve + jnp.sum(lanes.reshape(WINDOW // 8, 8, HEAD_DIM), axis=0)

    red_z[z, 0:8] = curve
    red_z[z, 8:16] = residual_part

    def red_copy(buf, here, n, base, device):
        return remote(buf.at[here], buf.at[here], red_send.at[n], red_recv.at[base + here], device)

    def red_arrival(buf, there, base):
        return remote(buf.at[there], buf.at[there], red_send.at[0], red_recv.at[base + there], dev_pair)

    for i in range(1, n_z):
        other = lax.rem(z + i, n_z)
        red_copy(red_z, z, i, 0, (group, at_ctx(other, x_lo, core))).start()

    def c_copy(h_):
        return remote(
            cout.at[:, head_cols(h_)], cin.at[x_lo, group],
            c_send.at[h_], c_recv.at[x_lo * n_group + group],
            (h_ // 2, at_ctx(z, h_ % 2, core)),
        )

    def c_arrival(x_lo_, group_):
        return remote(
            cout.at[:, head_cols(0)], cin.at[x_lo_, group_],
            c_send.at[0], c_recv.at[x_lo_ * n_group + group_], dev_pair,
        )

    block = 512
    for n in range(n_heads * HEAD_DIM // block):
        at = slice(n * block, (n + 1) * block)
        cout[:, at] = dot_nt(plow[...], wbuf[at]).astype(BF16)

        for h_ in range(n * (block // HEAD_DIM), (n + 1) * (block // HEAD_DIM)):

            @pl.when(h_ != head)
            def _():
                c_copy(h_).start()

    cin[x_lo, group] = cout[:, head_cols(head)]

    t_copy(group, 1 - x_lo, 0).wait_send()
    for i in range(2, n_heads):
        t_copy(0, 0, i).wait_send()

    for i in range(1, n_group):
        c_arrival(x_lo, lax.rem(group + i, n_group)).wait_recv()
    for i in range(n_group):
        c_arrival(1 - x_lo, i).wait_recv()

    starts = [((both // 16 - 3) * i + 3) // (n_group - 1) * 16 for i in range(n_group)]
    for i in range(n_group):
        cbuf[starts[i] : starts[i] + WINDOW] = (
            cin[0, i].astype(F32) + cin[1, i].astype(F32)
        ).astype(BF16)

    def backward(first_unit, block_rows):
        cot = cbuf[block_rows]
        centering = jnp.sum(cot.astype(F32) * att[block_rows], axis=1, keepdims=True)
        final = high[block_rows]
        units = [first_unit + i for i in range(4)]
        backs = [dot_nt(cot, vb[unit_rows(h)]) for h in units]
        total = None
        for h, back in zip(units, backs):
            grad = (pw[h, block_rows].astype(F32) * (back - centering)).astype(BF16)
            factor = jnp.exp2((highs[h, block_rows] - final) * EXP2_SCALE)
            product = dot_nn(grad, kb[unit_rows(h)]) * factor
            total = product if total is None else total + product
        qg[block_rows] += total

    def scaled(block_rows):
        return qg[block_rows] * (SCALING / acc[block_rows, HEAD_DIM : 2 * HEAD_DIM])

    @pl.loop(0, n_units // 8)
    def _(i):
        backward(4 * i, other_rows)

    for i in range(1, n_z):
        red_arrival(red_z, lax.rem(z + i, n_z), 0).wait_recv()
    red_g[head] = jnp.sum(red_z[...], axis=0)
    for i in range(1, n_heads):
        other = lax.rem(head + i, n_heads)
        device = (lax.div(other, 2), at_ctx(z, lax.rem(other, 2), core))
        red_copy(red_g, head, n_z + i, n_z, device).start()

    @pl.loop(n_units // 8, n_units // 4)
    def _(i):
        backward(4 * i, other_rows)

    qg[other_rows] = scaled(other_rows)
    back_copy = remote(
        qg.at[other_rows], qg_in, back_send.at[0], back_recv.at[0], dev_pair
    )
    back_copy.start()

    @pl.loop(0, n_units // 4)
    def _(i):
        backward(4 * i, own_rows)


    for i in range(1, n_heads):
        red_arrival(red_g, lax.rem(head + i, n_heads), n_z).wait_recv()
    red_c[core] = jnp.sum(red_g[...], axis=0)
    last = red_copy(red_c, core, n_z + n_heads, n_z + n_heads, dev_sib)
    last.start()
    for i in range(1, n_z):
        red_copy(red_z, z, i, 0, dev_next).wait_send()
    for i in range(1, n_heads):
        red_copy(red_g, head, n_z + i, n_z, dev_pair).wait_send()
    for h_ in range(n_heads):

        @pl.when(h_ != head)
        def _():
            c_copy(h_).wait_send()

    red_arrival(red_c, 1 - core, n_z + n_heads).wait_recv()
    last.wait_send()
    sums = jnp.sum(red_c[...], axis=0)
    curvature = jnp.sum(jnp.sum(sums[0:8], axis=0, keepdims=True), axis=1, keepdims=True)
    residual_sq = jnp.sum(jnp.sum(sums[8:16], axis=0, keepdims=True), axis=1, keepdims=True)
    step_size = residual_sq / curvature
    out_ref[:, own_cols] = dirb[:, own_cols].astype(F32) - step_size * scaled(own_rows)
    back_copy.wait_recv()
    out_ref[:, other_cols] = dirb[:, other_cols].astype(F32) - step_size * qg_in[...]
    back_copy.wait_send()


def body(n_group, n_z, queries, key_rows, value_rows, query_dir, out_weight):
    rows = queries.shape[0]
    both, unit = 2 * rows, 4 * rows
    width = out_weight.shape[1]
    n_heads = 2 * n_group
    any_spec = pl.BlockSpec(memory_space=pl.ANY)
    dma = pltpu.SemaphoreType.DMA
    n_red = n_z + n_heads + 2
    return pl.pallas_call(
        functools.partial(kernel, n_group, n_z, rows),
        out_shape=jax.ShapeDtypeStruct((rows, 2 * HEAD_DIM), F32),
        in_specs=[any_spec] * 5,
        out_specs=pl.BlockSpec(memory_space=pltpu.VMEM),
        scratch_shapes=[
            pltpu.VMEM((n_z * unit, HEAD_DIM), BF16),
            pltpu.VMEM((n_z * unit, HEAD_DIM), BF16),
            pltpu.VMEM((2 * both, HEAD_DIM), BF16),
            pltpu.VMEM((n_z, both, unit), BF16),
            pltpu.VMEM((n_z, both, 1), F32),
            pltpu.VMEM((both, 1), F32),
            pltpu.VMEM((2 * both, 2 * HEAD_DIM), F32),
            pltpu.VMEM((rows, 2 * HEAD_DIM), BF16),
            pltpu.VMEM((both, HEAD_DIM), F32),
            pltpu.VMEM((both, HEAD_DIM), BF16),
            pltpu.VMEM((WINDOW, n_heads * HEAD_DIM), BF16),
            pltpu.VMEM((n_heads * HEAD_DIM, width // 2), BF16),
            pltpu.VMEM((WINDOW, width // 2), BF16),
            pltpu.VMEM((WINDOW, n_heads * HEAD_DIM), BF16),
            pltpu.VMEM((2, n_group, WINDOW, HEAD_DIM), BF16),
            pltpu.VMEM((both, HEAD_DIM), BF16),
            pltpu.VMEM((both, HEAD_DIM), F32),
            pltpu.VMEM((rows, HEAD_DIM), F32),
            pltpu.VMEM((n_z, 16, HEAD_DIM), F32),
            pltpu.VMEM((n_heads, 16, HEAD_DIM), F32),
            pltpu.VMEM((2, 16, HEAD_DIM), F32),
            dma((6,)),
            dma((4,)), dma((4,)),
            dma((4 * n_z + 8,)), dma((4 * n_z + 8,)),
            dma((2 * n_z + 8,)), dma((2 * n_z + 8,)),
            dma((21,)), dma((21,)),
            dma((n_heads,)), dma((n_heads,)),
            dma((n_heads,)), dma((n_heads,)),
            dma((n_red,)), dma((n_red,)),
            dma((1,)), dma((1,)),
        ],
        compiler_params=pltpu.CompilerParams(
            collective_id=0, has_side_effects=True, vmem_limit_bytes=60 * 1024 * 1024
        ),
        name="gauss_newton_layer",
    )(queries, key_rows, value_rows, query_dir, out_weight)


def solution(mesh):
    n_group, n_ctx = mesh.shape["group"], mesh.shape["ctx"]
    in_specs = (
        P("ctx", "group"),
        P("ctx", "group"),
        P("ctx", "group"),
        P("ctx", "group"),
        P("group", None),
    )
    return jax.shard_map(
        functools.partial(body, n_group, n_ctx // (N_XLO * N_CORE)),
        mesh=mesh, in_specs=in_specs, out_specs=P("ctx", "group"), check_vma=False,
    )
```

```python
import functools
import math

import jax
import jax.numpy as jnp
from jax import lax
from jax.experimental import pallas as pl
from jax.experimental.pallas import tpu as pltpu
from jax.sharding import PartitionSpec as P

MESH = pl.DeviceIdType.MESH
HEAD_DIM = 128
SCALING = HEAD_DIM ** (-0.5)
EXP2_SCALE = SCALING * math.log2(math.e)
N_Y, N_XLO, N_CORE = 4, 2, 2
WINDOW = 48
F32, BF16 = jnp.float32, jnp.bfloat16


def dot_nt(a, b):
    return lax.dot_general(a, b, (((1,), (1,)), ((), ())), preferred_element_type=F32)


def dot_nn(a, b):
    return lax.dot_general(a, b, (((1,), (0,)), ((), ())), preferred_element_type=F32)


def kernel(
    n_group, n_z, rows,
    q_ref, k_ref, v_ref, d_ref, w_ref, out_ref,
    kv, qd, pw, highs, high, acc, dirb, att, tbuf, tin, wbuf, plow, cout, cin, cbuf, qg, qg_out, qg_in,
    red_z, red_g, red_c, curve_sum,
    local_sem, swap_send, swap_recv, ring_send, ring_recv, sib_send, sib_recv,
    w_send, w_recv, t_send, t_recv, c_send, c_recv, red_send, red_recv, back_send, back_recv,
):
    group, ctx = lax.axis_index("group"), lax.axis_index("ctx")
    x_hi, y = lax.div(group, N_Y), lax.rem(group, N_Y)
    z, x_lo, core = lax.div(ctx, 4), lax.rem(lax.div(ctx, 2), 2), lax.rem(ctx, 2)
    head = 2 * group + x_lo
    both = 2 * rows
    unit = 4 * rows
    half_z = n_z // 2
    n_heads = 2 * n_group
    wide = wbuf.shape[1]

    def at_ctx(z_, x_lo_, core_):
        return 4 * z_ + 2 * x_lo_ + core_

    z_next, z_prev = lax.rem(z + 1, n_z), lax.rem(z + n_z - 1, n_z)
    dev_next = (group, at_ctx(z_next, x_lo, core))
    dev_prev = (group, at_ctx(z_prev, x_lo, core))
    dev_sib = (group, at_ctx(z, x_lo, 1 - core))
    dev_pair = (group, at_ctx(z, 1 - x_lo, core))
    dev_across = ((1 - x_hi) * N_Y + y, at_ctx(z, 1 - x_lo, core))
    y_next, y_prev = lax.rem(y + 1, N_Y), lax.rem(y + N_Y - 1, N_Y)
    dev_up = (x_hi * N_Y + y_next, ctx)
    dev_down = (x_hi * N_Y + y_prev, ctx)

    def remote(src, dst, send, recv, device):
        return pltpu.make_async_remote_copy(
            src_ref=src, dst_ref=dst, send_sem=send, recv_sem=recv,
            device_id=device, device_id_type=MESH,
        )

    def part_of(o):
        return x_lo + o - 2 * x_lo * o

    def chunk_rows(p, core_, j):
        start = lax.div(p, 2) * (2 * unit) + j * unit + lax.rem(p, 2) * both + core_ * rows
        return pl.ds(pl.multiple_of(start, 16), rows)

    def chunk(p, core_, j):
        return kv.at[chunk_rows(p, core_, j)]

    own_cols = pl.ds(pl.multiple_of(x_lo * HEAD_DIM, HEAD_DIM), HEAD_DIM)
    other_cols = pl.ds(pl.multiple_of((1 - x_lo) * HEAD_DIM, HEAD_DIM), HEAD_DIM)
    own_rows = pl.ds(pl.multiple_of(x_lo * rows, 16), rows)
    other_rows = pl.ds(pl.multiple_of((1 - x_lo) * rows, 16), rows)
    own_tan = pl.ds(pl.multiple_of(both + x_lo * rows, 16), rows)
    other_tan = pl.ds(pl.multiple_of(both + (1 - x_lo) * rows, 16), rows)
    first = chunk_rows(0, core, x_lo)
    second = chunk_rows(0, core, 1 - x_lo)
    own_half = pl.ds(pl.multiple_of(x_lo * wide, 128), wide)
    other_half = pl.ds(pl.multiple_of((1 - x_lo) * wide, 128), wide)

    def w_rows(x_hi_, y_, piece):
        start = (x_hi_ * N_Y + y_) * 256 + piece * 128
        return pl.ds(pl.multiple_of(start, 128), 128)

    local = [
        pltpu.make_async_copy(k_ref.at[:, own_cols], kv.at[first, 0:HEAD_DIM], local_sem.at[0]),
        pltpu.make_async_copy(
            v_ref.at[:, own_cols], kv.at[first, HEAD_DIM : 2 * HEAD_DIM], local_sem.at[1]
        ),
        pltpu.make_async_copy(q_ref.at[:, own_cols], qd.at[own_rows], local_sem.at[2]),
        pltpu.make_async_copy(d_ref.at[:, own_cols], qd.at[own_tan], local_sem.at[3]),
        pltpu.make_async_copy(d_ref, dirb, local_sem.at[4]),
        pltpu.make_async_copy(
            w_ref.at[:, own_half],
            wbuf.at[pl.ds(pl.multiple_of(group * 256, 256), 256)],
            local_sem.at[5],
        ),
    ]
    for copy in local:
        copy.start()

    barrier = pltpu.get_barrier_semaphore()

    def greet(device):
        pl.semaphore_signal(barrier, inc=1, device_id=device, device_id_type=MESH)

    greet(dev_next)
    greet(dev_prev)
    greet(dev_sib)
    greet(dev_pair)
    for i in range(1, n_group):
        other = lax.rem(group + i, n_group)
        greet((other, at_ctx(z, x_lo, core)))
        greet((other, at_ctx(z, 1 - x_lo, core)))
    pl.semaphore_wait(barrier, 4 + 2 * (n_group - 1))

    swap = [
        remote(
            k_ref.at[:, other_cols], kv.at[first, 0:HEAD_DIM],
            swap_send.at[0], swap_recv.at[0], dev_pair,
        ),
        remote(
            v_ref.at[:, other_cols], kv.at[first, HEAD_DIM : 2 * HEAD_DIM],
            swap_send.at[1], swap_recv.at[1], dev_pair,
        ),
        remote(
            q_ref.at[:, other_cols], qd.at[own_rows], swap_send.at[2], swap_recv.at[2], dev_pair
        ),
        remote(
            d_ref.at[:, other_cols], qd.at[own_tan], swap_send.at[3], swap_recv.at[3], dev_pair
        ),
    ]
    swap_in = [
        remote(
            k_ref.at[:, other_cols], kv.at[second, 0:HEAD_DIM],
            swap_send.at[0], swap_recv.at[0], dev_pair,
        ),
        remote(
            v_ref.at[:, other_cols], kv.at[second, HEAD_DIM : 2 * HEAD_DIM],
            swap_send.at[1], swap_recv.at[1], dev_pair,
        ),
        remote(
            q_ref.at[:, other_cols], qd.at[other_rows], swap_send.at[2], swap_recv.at[2], dev_pair
        ),
        remote(
            d_ref.at[:, other_cols], qd.at[other_tan], swap_send.at[3], swap_recv.at[3], dev_pair
        ),
    ]
    swap[0].start()
    swap[1].start()

    def ring(way, s, o, f, src_p, dst_p):
        j = part_of(o)
        cols = slice(f * HEAD_DIM, (f + 1) * HEAD_DIM)
        return remote(
            kv.at[chunk_rows(src_p, core, j), cols], kv.at[chunk_rows(dst_p, core, j), cols],
            ring_send.at[way, s - 1, o, f], ring_recv.at[way, s - 1, o, f],
            dev_next if way == 0 else dev_prev,
        )

    def sibling(p, o, core_):
        place = chunk(p, core_, part_of(o))
        return remote(place, place, sib_send.at[p, o], sib_recv.at[p, o], dev_sib)

    local[0].wait()
    local[1].wait()
    for f in range(2):
        ring(0, 1, 0, f, 0, 1).start()
        ring(1, 1, 0, f, 0, 2).start()
    swap[2].start()
    swap[3].start()
    sibling(0, 0, core).start()

    def w_copy(n, src, dst, device):
        return remote(src, dst, w_send.at[n], w_recv.at[n], device)

    def w_piece(x_hi_, y_, piece):
        return wbuf.at[w_rows(x_hi_, y_, piece)]

    def w_half(x_hi_, y_, part):
        start = (x_hi_ * N_Y + y_) * 256 + core * 128 + part * 64
        return wbuf.at[pl.ds(pl.multiple_of(start, 64), 64)]

    own_w = w_piece(x_hi, y, core)
    across_w = w_piece(1 - x_hi, y, core)
    y_far = lax.rem(y + 2, N_Y)
    w_src = w_ref.at[pl.ds(pl.multiple_of(core * 128, 128), 128), other_half]
    local[5].wait()
    w_copy(0, w_src, own_w, dev_across).start()
    w_copy(1, own_w, own_w, dev_up).start()
    w_copy(2, own_w, own_w, dev_down).start()

    for f in range(2):
        swap_in[f].wait_recv()
        ring(0, 1, 1, f, 0, 1).start()
        ring(1, 1, 1, f, 0, 2).start()
    sibling(0, 1, core).start()

    def w_sibling(n, x_hi_, y_, core_):
        place = w_piece(x_hi_, y_, core_)
        return w_copy(n, place, place, dev_sib)

    def w_middle():
        w_copy(0, across_w, across_w, dev_across).wait_recv()
        w_copy(5, across_w, across_w, dev_up).start()
        w_copy(6, across_w, across_w, dev_down).start()
        below, above = w_piece(x_hi, y_prev, core), w_piece(x_hi, y_next, core)
        w_copy(1, below, below, dev_up).wait_recv()
        onward = w_half(x_hi, y_prev, 0)
        w_copy(3, onward, onward, dev_up).start()
        w_copy(2, above, above, dev_down).wait_recv()
        onward = w_half(x_hi, y_next, 1)
        w_copy(4, onward, onward, dev_down).start()
        w_sibling(9, 1 - x_hi, y, core).start()
        w_sibling(10, x_hi, y_prev, core).start()
        w_sibling(11, x_hi, y_next, core).start()

    def w_late():
        below, above = w_piece(1 - x_hi, y_prev, core), w_piece(1 - x_hi, y_next, core)
        w_copy(5, below, below, dev_up).wait_recv()
        onward = w_half(1 - x_hi, y_prev, 0)
        w_copy(7, onward, onward, dev_up).start()
        w_copy(6, above, above, dev_down).wait_recv()
        onward = w_half(1 - x_hi, y_next, 1)
        w_copy(8, onward, onward, dev_down).start()
        w_sibling(13, 1 - x_hi, y_prev, core).start()
        w_sibling(14, 1 - x_hi, y_next, core).start()
        place = w_half(x_hi, y_far, 0)
        w_copy(3, place, place, dev_up).wait_recv()
        place = w_half(x_hi, y_far, 1)
        w_copy(4, place, place, dev_down).wait_recv()
        w_sibling(12, x_hi, y_far, core).start()

    def w_sent():
        for copy in swap:
            copy.wait_send()
        for n in (0, 1, 2, 5, 6):
            w_copy(n, own_w, own_w, dev_up).wait_send()
        for n in (3, 4):
            w_copy(n, w_half(x_hi, y, 0), w_half(x_hi, y, 0), dev_up).wait_send()
        for n in range(9, 15):
            w_sibling(n, x_hi, y, core).wait_send()

    def w_last():
        place = w_half(1 - x_hi, y_far, 0)
        w_copy(7, place, place, dev_up).wait_recv()
        place = w_half(1 - x_hi, y_far, 1)
        w_copy(8, place, place, dev_down).wait_recv()
        w_sibling(15, 1 - x_hi, y_far, core).start()

    def w_finish():
        w_sibling(9, 1 - x_hi, y, 1 - core).wait_recv()
        w_sibling(10, x_hi, y_prev, 1 - core).wait_recv()
        w_sibling(11, x_hi, y_next, 1 - core).wait_recv()
        w_sibling(12, x_hi, y_far, 1 - core).wait_recv()
        w_sibling(13, 1 - x_hi, y_prev, 1 - core).wait_recv()
        w_sibling(14, 1 - x_hi, y_next, 1 - core).wait_recv()
        w_sibling(15, 1 - x_hi, y_far, 1 - core).wait_recv()

    high[...] = jnp.full(high.shape, -1e30, F32)
    acc[...] = jnp.zeros(acc.shape, F32)
    qg[...] = jnp.zeros(qg.shape, F32)
    def service(h):
        b, o = lax.div(h, 2), lax.rem(h, 2)
        s = b + 1
        back_p, ahead_p = 2 * s - 1, 2 * s

        @pl.when(s + 1 < half_z)
        def _():
            for f in range(2):
                ring(0, s, o, f, back_p, back_p).wait_recv()
                ring(0, s + 1, o, f, back_p, back_p + 2).start()
                ring(1, s, o, f, ahead_p, ahead_p).wait_recv()
                ring(1, s + 1, o, f, ahead_p, ahead_p + 2).start()

        @pl.when(s + 1 == half_z)
        def _():
            for f in range(2):
                ring(0, s, o, f, back_p, back_p).wait_recv()

                @pl.when(o == 0)
                def _():
                    ring(0, s + 1, o, f, back_p, back_p + 2).start()

                ring(1, s, o, f, ahead_p, ahead_p).wait_recv()

                @pl.when(o == 1)
                def _():
                    ring(1, s + 1, o, f, ahead_p, n_z - 1).start()

        @pl.when(s < half_z)
        def _():
            sibling(back_p, o, core).start()
            sibling(ahead_p, o, core).start()

        @pl.when(s == half_z)
        def _():
            for f in range(2):

                @pl.when(o == 0)
                def _():
                    ring(0, s, o, f, back_p, back_p).wait_recv()

                @pl.when(o == 1)
                def _():
                    ring(1, s, o, f, back_p, back_p).wait_recv()

            sibling(back_p, o, core).start()

        @pl.when(s >= 2)
        def _():
            for f in range(2):
                ring(0, s - 1, o, f, 1, 1).wait_send()
                ring(1, s - 1, o, f, 1, 1).wait_send()
            sibling(2 * s - 3, o, core).wait_send()
            sibling(2 * s - 2, o, core).wait_send()

    def unit_rows(h):
        start = lax.div(h, 2) * (2 * unit) + part_of(lax.rem(h, 2)) * unit
        return pl.ds(pl.multiple_of(start, 16), unit)

    ones = jnp.ones((unit, HEAD_DIM), BF16)

    def forward(h):
        b, o = lax.div(h, 2), lax.rem(h, 2)

        @pl.when(b == 0)
        def _():
            sibling(0, o, 1 - core).wait_recv()

        sibling(2 * b + 1, o, 1 - core).wait_recv()

        @pl.when(b + 1 < half_z)
        def _():
            sibling(2 * b + 2, o, 1 - core).wait_recv()

        here = unit_rows(h)
        keys = kv[here, 0:HEAD_DIM]
        values = kv[here, HEAD_DIM : 2 * HEAD_DIM]
        scores = dot_nt(qd[0:both], keys)
        tangents = dot_nt(qd[both : 2 * both], keys)
        old = high[...]
        new = jnp.maximum(old, jnp.max(scores, axis=1, keepdims=True))
        high[...] = new
        highs[h] = new
        factor = jnp.exp2((old - new) * EXP2_SCALE)
        weights = jnp.exp2((scores - new) * EXP2_SCALE)
        weighted = weights * tangents
        pw[h, 0:both] = weights.astype(BF16)
        pw[h, both : 2 * both] = weighted.astype(BF16)
        mixed = dot_nn(pw[h], jnp.concatenate([values, ones], axis=1))
        acc[0:both] = acc[0:both] * factor + mixed[0:both]
        acc[both : 2 * both] = acc[both : 2 * both] * factor + mixed[both : 2 * both]

    n_units = n_z
    service(0)
    for copy in local[2:5]:
        copy.wait()
    swap_in[2].wait_recv()
    swap_in[3].wait_recv()
    direction = dirb[...].astype(F32)
    squares = jnp.sum((direction * direction).reshape(rows // 8, 8, 2 * HEAD_DIM), axis=0)
    residual_part = squares[:, :HEAD_DIM] + squares[:, HEAD_DIM:]

    @pl.loop(1, n_units + 1)
    def _(h):
        @pl.when(h < n_units)
        def _():
            service(h)

        @pl.when(h == 5)
        def _():
            w_middle()

        @pl.when(h == 12)
        def _():
            w_late()

        @pl.when(h == 14)
        def _():
            w_sent()

        @pl.when(h == n_units)
        def _():
            w_last()

        forward(h - 1)

    totals = acc[0:both, HEAD_DIM : 2 * HEAD_DIM]
    attended = acc[0:both, 0:HEAD_DIM] / totals
    tbuf[...] = (
        (acc[both : 2 * both, 0:HEAD_DIM] - acc[both : 2 * both, HEAD_DIM : 2 * HEAD_DIM] * attended)
        * (SCALING / totals)
    ).astype(BF16)

    def window_start(i):
        return lax.div(((both // 16 - 3) * i + 3), n_group - 1) * 16

    def window(i):
        return pl.ds(pl.multiple_of(window_start(i), 16), WINDOW)

    def head_cols(h_):
        return pl.ds(pl.multiple_of(h_ * HEAD_DIM, HEAD_DIM), HEAD_DIM)

    def t_copy(group_, x_lo_, slot):
        return remote(
            tbuf.at[window(group_)], tin.at[:, head_cols(head)],
            t_send.at[slot], t_recv.at[head], (group_, at_ctx(z, x_lo_, core)),
        )

    def t_arrival(h_):
        return remote(
            tbuf.at[window(0)], tin.at[:, head_cols(h_)], t_send.at[0], t_recv.at[h_], dev_pair
        )

    t_copy(group, 1 - x_lo, 0).start()
    for i in range(1, n_group):
        other = lax.rem(group + i, n_group)
        t_copy(other, x_lo, 2 * i).start()
        t_copy(other, 1 - x_lo, 2 * i + 1).start()

    tin[:, head_cols(head)] = tbuf[window(group)]
    att[...] = attended
    w_finish()

    for f in range(2):
        ring(0, half_z, 0, f, 1, 1).wait_send()
        ring(1, half_z, 1, f, 1, 1).wait_send()
    for o in range(2):
        sibling(0, o, core).wait_send()
        sibling(n_z - 1, o, core).wait_send()
    for n in (7, 8):
        w_copy(n, w_half(x_hi, y, 0), w_half(x_hi, y, 0), dev_up).wait_send()
    w_sibling(15, x_hi, y, core).wait_send()

    for i in range(1, n_heads):
        t_arrival(lax.rem(head + i, n_heads)).wait_recv()

    counted = window_start(group + 1) - window_start(group)
    row_id = lax.broadcasted_iota(jnp.int32, (WINDOW, HEAD_DIM), 0)
    step = wide // 3
    curve_sum[...] = jnp.zeros(curve_sum.shape, F32)

    @pl.loop(0, 3)
    def _(n):
        cols = pl.ds(pl.multiple_of(n * step, 128), step)
        proj = dot_nn(tin[...], wbuf[:, cols])
        plow[:, cols] = proj.astype(BF16)
        squared = proj * proj
        lanes = squared[:, 0:HEAD_DIM]
        for m in range(1, step // HEAD_DIM):
            lanes = lanes + squared[:, m * HEAD_DIM : (m + 1) * HEAD_DIM]
        lanes = jnp.where(row_id < counted, lanes, 0.0)
        curve_sum[...] += jnp.sum(lanes.reshape(WINDOW // 8, 8, HEAD_DIM), axis=0)

    red_z[z, 0:8] = curve_sum[...]
    red_z[z, 8:16] = residual_part

    def red_copy(buf, here, n, base, device):
        return remote(buf.at[here], buf.at[here], red_send.at[n], red_recv.at[base + here], device)

    def red_arrival(buf, there, base):
        return remote(buf.at[there], buf.at[there], red_send.at[0], red_recv.at[base + there], dev_pair)

    for i in range(1, n_z):
        other = lax.rem(z + i, n_z)
        red_copy(red_z, z, i, 0, (group, at_ctx(other, x_lo, core))).start()

    def c_copy(h_):
        return remote(
            cout.at[:, head_cols(h_)], cin.at[x_lo, group],
            c_send.at[h_], c_recv.at[x_lo * n_group + group],
            (lax.div(h_, 2), at_ctx(z, lax.rem(h_, 2), core)),
        )

    def c_arrival(x_lo_, group_):
        return remote(
            cout.at[:, head_cols(0)], cin.at[x_lo_, group_],
            c_send.at[0], c_recv.at[x_lo_ * n_group + group_], dev_pair,
        )

    block = 512

    @pl.loop(0, n_heads * HEAD_DIM // block)
    def _(n):
        at = pl.ds(pl.multiple_of(n * block, block), block)
        cout[:, at] = dot_nt(plow[...], wbuf[at]).astype(BF16)

        for i in range(block // HEAD_DIM):
            h_ = n * (block // HEAD_DIM) + i

            @pl.when(h_ != head)
            def _():
                c_copy(h_).start()

    cin[x_lo, group] = cout[:, head_cols(head)]

    t_copy(group, 1 - x_lo, 0).wait_send()
    for i in range(2, n_heads):
        t_copy(0, 0, i).wait_send()

    for i in range(1, n_group):
        c_arrival(x_lo, lax.rem(group + i, n_group)).wait_recv()
    for i in range(n_group):
        c_arrival(1 - x_lo, i).wait_recv()

    starts = [((both // 16 - 3) * i + 3) // (n_group - 1) * 16 for i in range(n_group)]
    for i in range(n_group):
        cbuf[starts[i] : starts[i] + WINDOW] = (
            cin[0, i].astype(F32) + cin[1, i].astype(F32)
        ).astype(BF16)

    def backward(first_unit, block_rows):
        cot = cbuf[block_rows]
        centering = jnp.sum(cot.astype(F32) * att[block_rows], axis=1, keepdims=True)
        final = high[block_rows]
        units = [first_unit + i for i in range(4)]
        backs = [dot_nt(cot, kv[unit_rows(h), HEAD_DIM : 2 * HEAD_DIM]) for h in units]
        total = None
        for h, back in zip(units, backs):
            grad = (pw[h, block_rows].astype(F32) * (back - centering)).astype(BF16)
            factor = jnp.exp2((highs[h, block_rows] - final) * EXP2_SCALE)
            product = dot_nn(grad, kv[unit_rows(h), 0:HEAD_DIM]) * factor
            total = product if total is None else total + product
        qg[block_rows] += total

    def scaled(block_rows):
        return qg[block_rows] * (SCALING / acc[block_rows, HEAD_DIM : 2 * HEAD_DIM])

    back_copy = remote(qg_out, qg_in, back_send.at[0], back_recv.at[0], dev_pair)
    last = red_copy(red_c, core, n_z + n_heads, n_z + n_heads, dev_sib)
    per_half = n_units // 4

    for i in range(1, n_z):
        red_arrival(red_z, lax.rem(z + i, n_z), 0).wait_recv()
    red_g[head] = jnp.sum(red_z[...], axis=0)
    for i in range(1, n_heads):
        other = lax.rem(head + i, n_heads)
        device = (lax.div(other, 2), at_ctx(z, lax.rem(other, 2), core))
        red_copy(red_g, head, n_z + i, n_z, device).start()

    @pl.loop(0, 2 * per_half)
    def _(i):
        mine = lax.div(i, per_half)
        side = 1 - x_lo + mine * (2 * x_lo - 1)
        backward(
            4 * (i - mine * per_half), pl.ds(pl.multiple_of(side * rows, 16), rows)
        )

        @pl.when(i == per_half - 1)
        def _():
            qg_out[...] = scaled(other_rows).astype(BF16)
            back_copy.start()

        @pl.when(i == 2 * per_half - 2)
        def _():
            for i in range(1, n_heads):
                red_arrival(red_g, lax.rem(head + i, n_heads), n_z).wait_recv()
            red_c[core] = jnp.sum(red_g[...], axis=0)
            last.start()

    for i in range(1, n_z):
        red_copy(red_z, z, i, 0, dev_next).wait_send()
    for i in range(1, n_heads):
        red_copy(red_g, head, n_z + i, n_z, dev_pair).wait_send()
    for h_ in range(n_heads):

        @pl.when(h_ != head)
        def _():
            c_copy(h_).wait_send()

    red_arrival(red_c, 1 - core, n_z + n_heads).wait_recv()
    last.wait_send()
    sums = jnp.sum(red_c[...], axis=0)
    curvature = jnp.sum(jnp.sum(sums[0:8], axis=0, keepdims=True), axis=1, keepdims=True)
    residual_sq = jnp.sum(jnp.sum(sums[8:16], axis=0, keepdims=True), axis=1, keepdims=True)
    step_size = residual_sq / curvature
    out_ref[:, own_cols] = dirb[:, own_cols].astype(F32) - step_size * scaled(own_rows)
    back_copy.wait_recv()
    out_ref[:, other_cols] = dirb[:, other_cols].astype(F32) - step_size * qg_in[...].astype(F32)
    back_copy.wait_send()


def body(n_group, n_z, queries, key_rows, value_rows, query_dir, out_weight):
    rows = queries.shape[0]
    both, unit = 2 * rows, 4 * rows
    width = out_weight.shape[1]
    n_heads = 2 * n_group
    any_spec = pl.BlockSpec(memory_space=pl.ANY)
    dma = pltpu.SemaphoreType.DMA
    n_red = n_z + n_heads + 2
    return pl.pallas_call(
        functools.partial(kernel, n_group, n_z, rows),
        out_shape=jax.ShapeDtypeStruct((rows, 2 * HEAD_DIM), F32),
        in_specs=[any_spec] * 5,
        out_specs=pl.BlockSpec(memory_space=pltpu.VMEM),
        scratch_shapes=[
            pltpu.VMEM((n_z * unit, 2 * HEAD_DIM), BF16),
            pltpu.VMEM((2 * both, HEAD_DIM), BF16),
            pltpu.VMEM((n_z, 2 * both, unit), BF16),
            pltpu.VMEM((n_z, both, 1), F32),
            pltpu.VMEM((both, 1), F32),
            pltpu.VMEM((2 * both, 2 * HEAD_DIM), F32),
            pltpu.VMEM((rows, 2 * HEAD_DIM), BF16),
            pltpu.VMEM((both, HEAD_DIM), F32),
            pltpu.VMEM((both, HEAD_DIM), BF16),
            pltpu.VMEM((WINDOW, n_heads * HEAD_DIM), BF16),
            pltpu.VMEM((n_heads * HEAD_DIM, width // 2), BF16),
            pltpu.VMEM((WINDOW, width // 2), BF16),
            pltpu.VMEM((WINDOW, n_heads * HEAD_DIM), BF16),
            pltpu.VMEM((2, n_group, WINDOW, HEAD_DIM), BF16),
            pltpu.VMEM((both, HEAD_DIM), BF16),
            pltpu.VMEM((both, HEAD_DIM), F32),
            pltpu.VMEM((rows, HEAD_DIM), BF16),
            pltpu.VMEM((rows, HEAD_DIM), BF16),
            pltpu.VMEM((n_z, 16, HEAD_DIM), F32),
            pltpu.VMEM((n_heads, 16, HEAD_DIM), F32),
            pltpu.VMEM((2, 16, HEAD_DIM), F32),
            pltpu.VMEM((8, HEAD_DIM), F32),
            dma((6,)),
            dma((4,)), dma((4,)),
            dma((2, n_z // 2, 2, 2)), dma((2, n_z // 2, 2, 2)),
            dma((n_z, 2)), dma((n_z, 2)),
            dma((16,)), dma((16,)),
            dma((n_heads,)), dma((n_heads,)),
            dma((n_heads,)), dma((n_heads,)),
            dma((n_red,)), dma((n_red,)),
            dma((1,)), dma((1,)),
        ],
        compiler_params=pltpu.CompilerParams(
            collective_id=0, has_side_effects=True, vmem_limit_bytes=60 * 1024 * 1024
        ),
        name="gauss_newton_layer",
    )(queries, key_rows, value_rows, query_dir, out_weight)


def solution(mesh):
    n_group, n_ctx = mesh.shape["group"], mesh.shape["ctx"]
    in_specs = (
        P("ctx", "group"),
        P("ctx", "group"),
        P("ctx", "group"),
        P("ctx", "group"),
        P("group", None),
    )
    return jax.shard_map(
        functools.partial(body, n_group, n_ctx // (N_XLO * N_CORE)),
        mesh=mesh, in_specs=in_specs, out_specs=P("ctx", "group"), check_vma=False,
    )
```

```python
import functools
import math

import jax
import jax.numpy as jnp
from jax import lax
from jax.experimental import pallas as pl
from jax.experimental.pallas import tpu as pltpu
from jax.sharding import PartitionSpec as P

MESH = pl.DeviceIdType.MESH
HEAD_DIM = 128
SCALING = HEAD_DIM ** (-0.5)
EXP2_SCALE = SCALING * math.log2(math.e)
N_Y, N_XLO, N_CORE = 4, 2, 2
WINDOW = 48
F32, BF16 = jnp.float32, jnp.bfloat16


def dot_nt(a, b):
    return lax.dot_general(a, b, (((1,), (1,)), ((), ())), preferred_element_type=F32)


def dot_nn(a, b):
    return lax.dot_general(a, b, (((1,), (0,)), ((), ())), preferred_element_type=F32)


def kernel(
    n_group, n_z, rows,
    q_ref, k_ref, v_ref, d_ref, w_ref, out_ref,
    kv, qd, pw, highs, high, acc, dirb, att, tbuf, tin, wbuf, plow, cout, cin, cbuf, qg, qg_out, qg_in,
    red_z, red_g, red_c, curve_sum,
    local_sem, swap_send, swap_recv, ring_send, ring_recv, sib_send, sib_recv,
    w_send, w_recv, t_send, t_recv, c_send, c_recv, red_send, red_recv, back_send, back_recv,
):
    group, ctx = lax.axis_index("group"), lax.axis_index("ctx")
    x_hi, y = lax.div(group, N_Y), lax.rem(group, N_Y)
    z, x_lo, core = lax.div(ctx, 4), lax.rem(lax.div(ctx, 2), 2), lax.rem(ctx, 2)
    head = 2 * group + x_lo
    both = 2 * rows
    unit = 4 * rows
    half_z = n_z // 2
    n_heads = 2 * n_group
    wide = wbuf.shape[1]

    def at_ctx(z_, x_lo_, core_):
        return 4 * z_ + 2 * x_lo_ + core_

    z_next, z_prev = lax.rem(z + 1, n_z), lax.rem(z + n_z - 1, n_z)
    dev_next = (group, at_ctx(z_next, x_lo, core))
    dev_prev = (group, at_ctx(z_prev, x_lo, core))
    dev_sib = (group, at_ctx(z, x_lo, 1 - core))
    dev_pair = (group, at_ctx(z, 1 - x_lo, core))
    dev_across = ((1 - x_hi) * N_Y + y, at_ctx(z, 1 - x_lo, core))
    y_next, y_prev = lax.rem(y + 1, N_Y), lax.rem(y + N_Y - 1, N_Y)
    dev_up = (x_hi * N_Y + y_next, ctx)
    dev_down = (x_hi * N_Y + y_prev, ctx)

    def remote(src, dst, send, recv, device):
        return pltpu.make_async_remote_copy(
            src_ref=src, dst_ref=dst, send_sem=send, recv_sem=recv,
            device_id=device, device_id_type=MESH,
        )

    def part_of(o):
        return x_lo + o - 2 * x_lo * o

    def chunk_rows(p, core_, j):
        start = lax.div(p, 2) * (2 * unit) + j * unit + lax.rem(p, 2) * both + core_ * rows
        return pl.ds(pl.multiple_of(start, 16), rows)

    def chunk(p, core_, j):
        return kv.at[chunk_rows(p, core_, j)]

    own_cols = pl.ds(pl.multiple_of(x_lo * HEAD_DIM, HEAD_DIM), HEAD_DIM)
    other_cols = pl.ds(pl.multiple_of((1 - x_lo) * HEAD_DIM, HEAD_DIM), HEAD_DIM)
    own_rows = pl.ds(pl.multiple_of(x_lo * rows, 16), rows)
    other_rows = pl.ds(pl.multiple_of((1 - x_lo) * rows, 16), rows)
    own_tan = pl.ds(pl.multiple_of(both + x_lo * rows, 16), rows)
    other_tan = pl.ds(pl.multiple_of(both + (1 - x_lo) * rows, 16), rows)
    first = chunk_rows(0, core, x_lo)
    second = chunk_rows(0, core, 1 - x_lo)
    own_half = pl.ds(pl.multiple_of(x_lo * wide, 128), wide)
    other_half = pl.ds(pl.multiple_of((1 - x_lo) * wide, 128), wide)

    def w_rows(x_hi_, y_, piece):
        start = (x_hi_ * N_Y + y_) * 256 + piece * 128
        return pl.ds(pl.multiple_of(start, 128), 128)

    local = [
        pltpu.make_async_copy(k_ref.at[:, own_cols], kv.at[first, 0:HEAD_DIM], local_sem.at[0]),
        pltpu.make_async_copy(
            v_ref.at[:, own_cols], kv.at[first, HEAD_DIM : 2 * HEAD_DIM], local_sem.at[1]
        ),
        pltpu.make_async_copy(q_ref.at[:, own_cols], qd.at[own_rows], local_sem.at[2]),
        pltpu.make_async_copy(d_ref.at[:, own_cols], qd.at[own_tan], local_sem.at[3]),
        pltpu.make_async_copy(d_ref, dirb, local_sem.at[4]),
        pltpu.make_async_copy(
            w_ref.at[:, own_half],
            wbuf.at[pl.ds(pl.multiple_of(group * 256, 256), 256)],
            local_sem.at[5],
        ),
    ]
    for copy in local:
        copy.start()

    barrier = pltpu.get_barrier_semaphore()

    def greet(device):
        pl.semaphore_signal(barrier, inc=1, device_id=device, device_id_type=MESH)

    greet(dev_next)
    greet(dev_prev)
    greet(dev_sib)
    greet(dev_pair)
    greet(dev_up)
    greet(dev_down)
    greet(dev_across)
    pl.semaphore_wait(barrier, 7)

    swap = [
        remote(
            k_ref.at[:, other_cols], kv.at[first, 0:HEAD_DIM],
            swap_send.at[0], swap_recv.at[0], dev_pair,
        ),
        remote(
            v_ref.at[:, other_cols], kv.at[first, HEAD_DIM : 2 * HEAD_DIM],
            swap_send.at[1], swap_recv.at[1], dev_pair,
        ),
        remote(
            q_ref.at[:, other_cols], qd.at[own_rows], swap_send.at[2], swap_recv.at[2], dev_pair
        ),
        remote(
            d_ref.at[:, other_cols], qd.at[own_tan], swap_send.at[3], swap_recv.at[3], dev_pair
        ),
    ]
    swap_in = [
        remote(
            k_ref.at[:, other_cols], kv.at[second, 0:HEAD_DIM],
            swap_send.at[0], swap_recv.at[0], dev_pair,
        ),
        remote(
            v_ref.at[:, other_cols], kv.at[second, HEAD_DIM : 2 * HEAD_DIM],
            swap_send.at[1], swap_recv.at[1], dev_pair,
        ),
        remote(
            q_ref.at[:, other_cols], qd.at[other_rows], swap_send.at[2], swap_recv.at[2], dev_pair
        ),
        remote(
            d_ref.at[:, other_cols], qd.at[other_tan], swap_send.at[3], swap_recv.at[3], dev_pair
        ),
    ]
    swap[0].start()
    swap[1].start()

    def ring(way, s, o, f, src_p, dst_p):
        j = part_of(o)
        cols = slice(f * HEAD_DIM, (f + 1) * HEAD_DIM)
        return remote(
            kv.at[chunk_rows(src_p, core, j), cols], kv.at[chunk_rows(dst_p, core, j), cols],
            ring_send.at[way, s - 1, o, f], ring_recv.at[way, s - 1, o, f],
            dev_next if way == 0 else dev_prev,
        )

    def sibling(p, o, core_):
        place = chunk(p, core_, part_of(o))
        return remote(place, place, sib_send.at[p, o], sib_recv.at[p, o], dev_sib)

    local[0].wait()
    local[1].wait()
    for f in range(2):
        ring(0, 1, 0, f, 0, 1).start()
        ring(1, 1, 0, f, 0, 2).start()
    swap[2].start()
    swap[3].start()
    sibling(0, 0, core).start()

    def w_copy(n, src, dst, device):
        return remote(src, dst, w_send.at[n], w_recv.at[n], device)

    def w_piece(x_hi_, y_, piece):
        return wbuf.at[w_rows(x_hi_, y_, piece)]

    def w_half(x_hi_, y_, part):
        start = (x_hi_ * N_Y + y_) * 256 + core * 128 + part * 64
        return wbuf.at[pl.ds(pl.multiple_of(start, 64), 64)]

    own_w = w_piece(x_hi, y, core)
    across_w = w_piece(1 - x_hi, y, core)
    y_far = lax.rem(y + 2, N_Y)
    w_src = w_ref.at[pl.ds(pl.multiple_of(core * 128, 128), 128), other_half]
    local[5].wait()
    w_copy(0, w_src, own_w, dev_across).start()
    w_copy(1, own_w, own_w, dev_up).start()
    w_copy(2, own_w, own_w, dev_down).start()

    for f in range(2):
        swap_in[f].wait_recv()
        ring(0, 1, 1, f, 0, 1).start()
        ring(1, 1, 1, f, 0, 2).start()
    sibling(0, 1, core).start()

    def w_sibling(n, x_hi_, y_, core_):
        place = w_piece(x_hi_, y_, core_)
        return w_copy(n, place, place, dev_sib)

    def w_middle():
        w_copy(0, across_w, across_w, dev_across).wait_recv()
        w_copy(5, across_w, across_w, dev_up).start()
        w_copy(6, across_w, across_w, dev_down).start()
        below, above = w_piece(x_hi, y_prev, core), w_piece(x_hi, y_next, core)
        w_copy(1, below, below, dev_up).wait_recv()
        onward = w_half(x_hi, y_prev, 0)
        w_copy(3, onward, onward, dev_up).start()
        w_copy(2, above, above, dev_down).wait_recv()
        onward = w_half(x_hi, y_next, 1)
        w_copy(4, onward, onward, dev_down).start()
        w_sibling(9, 1 - x_hi, y, core).start()
        w_sibling(10, x_hi, y_prev, core).start()
        w_sibling(11, x_hi, y_next, core).start()

    def w_late():
        below, above = w_piece(1 - x_hi, y_prev, core), w_piece(1 - x_hi, y_next, core)
        w_copy(5, below, below, dev_up).wait_recv()
        onward = w_half(1 - x_hi, y_prev, 0)
        w_copy(7, onward, onward, dev_up).start()
        w_copy(6, above, above, dev_down).wait_recv()
        onward = w_half(1 - x_hi, y_next, 1)
        w_copy(8, onward, onward, dev_down).start()
        w_sibling(13, 1 - x_hi, y_prev, core).start()
        w_sibling(14, 1 - x_hi, y_next, core).start()
        place = w_half(x_hi, y_far, 0)
        w_copy(3, place, place, dev_up).wait_recv()
        place = w_half(x_hi, y_far, 1)
        w_copy(4, place, place, dev_down).wait_recv()
        w_sibling(12, x_hi, y_far, core).start()

    def w_sent():
        for copy in swap:
            copy.wait_send()
        for n in (0, 1, 2, 5, 6):
            w_copy(n, own_w, own_w, dev_up).wait_send()
        for n in (3, 4):
            w_copy(n, w_half(x_hi, y, 0), w_half(x_hi, y, 0), dev_up).wait_send()
        for n in range(9, 15):
            w_sibling(n, x_hi, y, core).wait_send()

    def w_last():
        place = w_half(1 - x_hi, y_far, 0)
        w_copy(7, place, place, dev_up).wait_recv()
        place = w_half(1 - x_hi, y_far, 1)
        w_copy(8, place, place, dev_down).wait_recv()
        w_sibling(15, 1 - x_hi, y_far, core).start()

    def w_finish():
        w_sibling(9, 1 - x_hi, y, 1 - core).wait_recv()
        w_sibling(10, x_hi, y_prev, 1 - core).wait_recv()
        w_sibling(11, x_hi, y_next, 1 - core).wait_recv()
        w_sibling(12, x_hi, y_far, 1 - core).wait_recv()
        w_sibling(13, 1 - x_hi, y_prev, 1 - core).wait_recv()
        w_sibling(14, 1 - x_hi, y_next, 1 - core).wait_recv()
        w_sibling(15, 1 - x_hi, y_far, 1 - core).wait_recv()

    high[...] = jnp.full(high.shape, -1e30, F32)
    acc[...] = jnp.zeros(acc.shape, F32)
    qg[...] = jnp.zeros(qg.shape, F32)
    def service(h):
        b, o = lax.div(h, 2), lax.rem(h, 2)
        s = b + 1
        back_p, ahead_p = 2 * s - 1, 2 * s

        @pl.when(s + 1 < half_z)
        def _():
            for f in range(2):
                ring(0, s, o, f, back_p, back_p).wait_recv()
                ring(0, s + 1, o, f, back_p, back_p + 2).start()
                ring(1, s, o, f, ahead_p, ahead_p).wait_recv()
                ring(1, s + 1, o, f, ahead_p, ahead_p + 2).start()

        @pl.when(s + 1 == half_z)
        def _():
            for f in range(2):
                ring(0, s, o, f, back_p, back_p).wait_recv()

                @pl.when(o == 0)
                def _():
                    ring(0, s + 1, o, f, back_p, back_p + 2).start()

                ring(1, s, o, f, ahead_p, ahead_p).wait_recv()

                @pl.when(o == 1)
                def _():
                    ring(1, s + 1, o, f, ahead_p, n_z - 1).start()

        @pl.when(s < half_z)
        def _():
            sibling(back_p, o, core).start()
            sibling(ahead_p, o, core).start()

        @pl.when(s == half_z)
        def _():
            for f in range(2):

                @pl.when(o == 0)
                def _():
                    ring(0, s, o, f, back_p, back_p).wait_recv()

                @pl.when(o == 1)
                def _():
                    ring(1, s, o, f, back_p, back_p).wait_recv()

            sibling(back_p, o, core).start()

        @pl.when(s >= 2)
        def _():
            for f in range(2):
                ring(0, s - 1, o, f, 1, 1).wait_send()
                ring(1, s - 1, o, f, 1, 1).wait_send()
            sibling(2 * s - 3, o, core).wait_send()
            sibling(2 * s - 2, o, core).wait_send()

    def unit_rows(h):
        start = lax.div(h, 2) * (2 * unit) + part_of(lax.rem(h, 2)) * unit
        return pl.ds(pl.multiple_of(start, 16), unit)

    ones = jnp.ones((unit, HEAD_DIM), BF16)

    def forward(h):
        b, o = lax.div(h, 2), lax.rem(h, 2)

        @pl.when(b == 0)
        def _():
            sibling(0, o, 1 - core).wait_recv()

        sibling(2 * b + 1, o, 1 - core).wait_recv()

        @pl.when(b + 1 < half_z)
        def _():
            sibling(2 * b + 2, o, 1 - core).wait_recv()

        here = unit_rows(h)
        keys = kv[here, 0:HEAD_DIM]
        values = kv[here, HEAD_DIM : 2 * HEAD_DIM]
        scores = dot_nt(qd[0:both], keys)
        tangents = dot_nt(qd[both : 2 * both], keys)
        old = high[...]
        new = jnp.maximum(old, jnp.max(scores, axis=1, keepdims=True))
        high[...] = new
        highs[h] = new
        factor = jnp.exp2((old - new) * EXP2_SCALE)
        weights = jnp.exp2((scores - new) * EXP2_SCALE)
        weighted = weights * tangents
        pw[h, 0:both] = weights.astype(BF16)
        pw[h, both : 2 * both] = weighted.astype(BF16)
        mixed = dot_nn(pw[h], jnp.concatenate([values, ones], axis=1))
        acc[0:both] = acc[0:both] * factor + mixed[0:both]
        acc[both : 2 * both] = acc[both : 2 * both] * factor + mixed[both : 2 * both]

    n_units = n_z
    service(0)
    for copy in local[2:5]:
        copy.wait()
    swap_in[2].wait_recv()
    swap_in[3].wait_recv()
    direction = dirb[...].astype(F32)
    squares = jnp.sum((direction * direction).reshape(rows // 8, 8, 2 * HEAD_DIM), axis=0)
    residual_part = squares[:, :HEAD_DIM] + squares[:, HEAD_DIM:]

    @pl.loop(1, n_units + 1)
    def _(h):
        @pl.when(h < n_units)
        def _():
            service(h)

        @pl.when(h == 5)
        def _():
            w_middle()

        @pl.when(h == 12)
        def _():
            w_late()

        @pl.when(h == 14)
        def _():
            w_sent()

        @pl.when(h == n_units)
        def _():
            w_last()

        forward(h - 1)

    totals = acc[0:both, HEAD_DIM : 2 * HEAD_DIM]
    attended = acc[0:both, 0:HEAD_DIM] / totals
    tbuf[...] = (
        (acc[both : 2 * both, 0:HEAD_DIM] - acc[both : 2 * both, HEAD_DIM : 2 * HEAD_DIM] * attended)
        * (SCALING / totals)
    ).astype(BF16)

    def window_start(i):
        return lax.div(((both // 16 - 3) * i + 3), n_group - 1) * 16

    def window(i):
        return pl.ds(pl.multiple_of(window_start(i), 16), WINDOW)

    def head_cols(h_):
        return pl.ds(pl.multiple_of(h_ * HEAD_DIM, HEAD_DIM), HEAD_DIM)

    def t_copy(group_, x_lo_, slot):
        return remote(
            tbuf.at[window(group_)], tin.at[:, head_cols(head)],
            t_send.at[slot], t_recv.at[head], (group_, at_ctx(z, x_lo_, core)),
        )

    def t_arrival(h_):
        return remote(
            tbuf.at[window(0)], tin.at[:, head_cols(h_)], t_send.at[0], t_recv.at[h_], dev_pair
        )

    t_copy(group, 1 - x_lo, 0).start()
    for i in sorted(range(1, n_group), key=lambda i: (0, 2, 3, 2)[i % N_Y], reverse=True):
        other = lax.rem(group + i, n_group)
        t_copy(other, x_lo, 2 * i).start()
        t_copy(other, 1 - x_lo, 2 * i + 1).start()

    tin[:, head_cols(head)] = tbuf[window(group)]
    att[...] = attended
    w_finish()

    for f in range(2):
        ring(0, half_z, 0, f, 1, 1).wait_send()
        ring(1, half_z, 1, f, 1, 1).wait_send()
    for o in range(2):
        sibling(0, o, core).wait_send()
        sibling(n_z - 1, o, core).wait_send()
    for n in (7, 8):
        w_copy(n, w_half(x_hi, y, 0), w_half(x_hi, y, 0), dev_up).wait_send()
    w_sibling(15, x_hi, y, core).wait_send()

    for i in range(1, n_heads):
        t_arrival(lax.rem(head + i, n_heads)).wait_recv()

    counted = window_start(group + 1) - window_start(group)
    row_id = lax.broadcasted_iota(jnp.int32, (WINDOW, HEAD_DIM), 0)
    step = wide // 3
    curve_sum[...] = jnp.zeros(curve_sum.shape, F32)

    @pl.loop(0, 3)
    def _(n):
        cols = pl.ds(pl.multiple_of(n * step, 128), step)
        proj = dot_nn(tin[...], wbuf[:, cols])
        plow[:, cols] = proj.astype(BF16)
        squared = proj * proj
        lanes = squared[:, 0:HEAD_DIM]
        for m in range(1, step // HEAD_DIM):
            lanes = lanes + squared[:, m * HEAD_DIM : (m + 1) * HEAD_DIM]
        lanes = jnp.where(row_id < counted, lanes, 0.0)
        curve_sum[...] += jnp.sum(lanes.reshape(WINDOW // 8, 8, HEAD_DIM), axis=0)

    red_z[z, 0:8] = curve_sum[...]
    red_z[z, 8:16] = residual_part

    def red_copy(buf, here, n, base, device):
        return remote(buf.at[here], buf.at[here], red_send.at[n], red_recv.at[base + here], device)

    def red_arrival(buf, there, base):
        return remote(buf.at[there], buf.at[there], red_send.at[0], red_recv.at[base + there], dev_pair)

    for i in sorted(range(1, n_z), key=lambda i: -min(i, n_z - i)):
        other = lax.rem(z + i, n_z)
        red_copy(red_z, z, i, 0, (group, at_ctx(other, x_lo, core))).start()

    def c_copy(h_):
        return remote(
            cout.at[:, head_cols(h_)], cin.at[x_lo, group],
            c_send.at[h_], c_recv.at[x_lo * n_group + group],
            (lax.div(h_, 2), at_ctx(z, lax.rem(h_, 2), core)),
        )

    def c_arrival(x_lo_, group_):
        return remote(
            cout.at[:, head_cols(0)], cin.at[x_lo_, group_],
            c_send.at[0], c_recv.at[x_lo_ * n_group + group_], dev_pair,
        )

    block = 512

    @pl.loop(0, n_heads * HEAD_DIM // block)
    def _(n):
        at = pl.ds(pl.multiple_of(n * block, block), block)
        cout[:, at] = dot_nt(plow[...], wbuf[at]).astype(BF16)

        for i in range(block // HEAD_DIM):
            h_ = n * (block // HEAD_DIM) + i

            @pl.when(h_ != head)
            def _():
                c_copy(h_).start()

    cin[x_lo, group] = cout[:, head_cols(head)]

    t_copy(group, 1 - x_lo, 0).wait_send()
    for i in range(2, n_heads):
        t_copy(0, 0, i).wait_send()

    for i in range(1, n_group):
        c_arrival(x_lo, lax.rem(group + i, n_group)).wait_recv()
    for i in range(n_group):
        c_arrival(1 - x_lo, i).wait_recv()

    starts = [((both // 16 - 3) * i + 3) // (n_group - 1) * 16 for i in range(n_group)]
    for i in range(n_group):
        cbuf[starts[i] : starts[i] + WINDOW] = (
            cin[0, i].astype(F32) + cin[1, i].astype(F32)
        ).astype(BF16)

    def backward(first_unit, block_rows):
        cot = cbuf[block_rows]
        centering = jnp.sum(cot.astype(F32) * att[block_rows], axis=1, keepdims=True)
        final = high[block_rows]
        units = [first_unit + i for i in range(4)]
        backs = [dot_nt(cot, kv[unit_rows(h), HEAD_DIM : 2 * HEAD_DIM]) for h in units]
        total = None
        for h, back in zip(units, backs):
            grad = (pw[h, block_rows].astype(F32) * (back - centering)).astype(BF16)
            factor = jnp.exp2((highs[h, block_rows] - final) * EXP2_SCALE)
            product = dot_nn(grad, kv[unit_rows(h), 0:HEAD_DIM]) * factor
            total = product if total is None else total + product
        qg[block_rows] += total

    def scaled(block_rows):
        return qg[block_rows] * (SCALING / acc[block_rows, HEAD_DIM : 2 * HEAD_DIM])

    back_copy = remote(qg_out, qg_in, back_send.at[0], back_recv.at[0], dev_pair)
    last = red_copy(red_c, core, n_z + n_heads, n_z + n_heads, dev_sib)
    per_half = n_units // 4

    for i in range(1, n_z):
        red_arrival(red_z, lax.rem(z + i, n_z), 0).wait_recv()
    red_g[head] = jnp.sum(red_z[...], axis=0)
    for i in sorted(range(1, n_heads), key=lambda i: (0, 2, 3, 2)[i // 2 % N_Y], reverse=True):
        other = lax.rem(head + i, n_heads)
        device = (lax.div(other, 2), at_ctx(z, lax.rem(other, 2), core))
        red_copy(red_g, head, n_z + i, n_z, device).start()

    @pl.loop(0, 2 * per_half)
    def _(i):
        mine = lax.div(i, per_half)
        side = 1 - x_lo + mine * (2 * x_lo - 1)
        backward(
            4 * (i - mine * per_half), pl.ds(pl.multiple_of(side * rows, 16), rows)
        )

        @pl.when(i == per_half - 1)
        def _():
            qg_out[...] = scaled(other_rows).astype(BF16)
            back_copy.start()

        @pl.when(i == 2 * per_half - 2)
        def _():
            for i in range(1, n_heads):
                red_arrival(red_g, lax.rem(head + i, n_heads), n_z).wait_recv()
            red_c[core] = jnp.sum(red_g[...], axis=0)
            last.start()

    for i in range(1, n_z):
        red_copy(red_z, z, i, 0, dev_next).wait_send()
    for i in range(1, n_heads):
        red_copy(red_g, head, n_z + i, n_z, dev_pair).wait_send()
    for h_ in range(n_heads):

        @pl.when(h_ != head)
        def _():
            c_copy(h_).wait_send()

    red_arrival(red_c, 1 - core, n_z + n_heads).wait_recv()
    last.wait_send()
    sums = jnp.sum(red_c[...], axis=0)
    curvature = jnp.sum(jnp.sum(sums[0:8], axis=0, keepdims=True), axis=1, keepdims=True)
    residual_sq = jnp.sum(jnp.sum(sums[8:16], axis=0, keepdims=True), axis=1, keepdims=True)
    step_size = residual_sq / curvature
    out_ref[:, own_cols] = dirb[:, own_cols].astype(F32) - step_size * scaled(own_rows)
    back_copy.wait_recv()
    out_ref[:, other_cols] = dirb[:, other_cols].astype(F32) - step_size * qg_in[...].astype(F32)
    back_copy.wait_send()


def body(n_group, n_z, queries, key_rows, value_rows, query_dir, out_weight):
    rows = queries.shape[0]
    both, unit = 2 * rows, 4 * rows
    width = out_weight.shape[1]
    n_heads = 2 * n_group
    any_spec = pl.BlockSpec(memory_space=pl.ANY)
    dma = pltpu.SemaphoreType.DMA
    n_red = n_z + n_heads + 2
    return pl.pallas_call(
        functools.partial(kernel, n_group, n_z, rows),
        out_shape=jax.ShapeDtypeStruct((rows, 2 * HEAD_DIM), F32),
        in_specs=[any_spec] * 5,
        out_specs=pl.BlockSpec(memory_space=pltpu.VMEM),
        scratch_shapes=[
            pltpu.VMEM((n_z * unit, 2 * HEAD_DIM), BF16),
            pltpu.VMEM((2 * both, HEAD_DIM), BF16),
            pltpu.VMEM((n_z, 2 * both, unit), BF16),
            pltpu.VMEM((n_z, both, 1), F32),
            pltpu.VMEM((both, 1), F32),
            pltpu.VMEM((2 * both, 2 * HEAD_DIM), F32),
            pltpu.VMEM((rows, 2 * HEAD_DIM), BF16),
            pltpu.VMEM((both, HEAD_DIM), F32),
            pltpu.VMEM((both, HEAD_DIM), BF16),
            pltpu.VMEM((WINDOW, n_heads * HEAD_DIM), BF16),
            pltpu.VMEM((n_heads * HEAD_DIM, width // 2), BF16),
            pltpu.VMEM((WINDOW, width // 2), BF16),
            pltpu.VMEM((WINDOW, n_heads * HEAD_DIM), BF16),
            pltpu.VMEM((2, n_group, WINDOW, HEAD_DIM), BF16),
            pltpu.VMEM((both, HEAD_DIM), BF16),
            pltpu.VMEM((both, HEAD_DIM), F32),
            pltpu.VMEM((rows, HEAD_DIM), BF16),
            pltpu.VMEM((rows, HEAD_DIM), BF16),
            pltpu.VMEM((n_z, 16, HEAD_DIM), F32),
            pltpu.VMEM((n_heads, 16, HEAD_DIM), F32),
            pltpu.VMEM((2, 16, HEAD_DIM), F32),
            pltpu.VMEM((8, HEAD_DIM), F32),
            dma((6,)),
            dma((4,)), dma((4,)),
            dma((2, n_z // 2, 2, 2)), dma((2, n_z // 2, 2, 2)),
            dma((n_z, 2)), dma((n_z, 2)),
            dma((16,)), dma((16,)),
            dma((n_heads,)), dma((n_heads,)),
            dma((n_heads,)), dma((n_heads,)),
            dma((n_red,)), dma((n_red,)),
            dma((1,)), dma((1,)),
        ],
        compiler_params=pltpu.CompilerParams(
            collective_id=0, has_side_effects=True, vmem_limit_bytes=60 * 1024 * 1024
        ),
        name="gauss_newton_layer",
    )(queries, key_rows, value_rows, query_dir, out_weight)


def solution(mesh):
    n_group, n_ctx = mesh.shape["group"], mesh.shape["ctx"]
    in_specs = (
        P("ctx", "group"),
        P("ctx", "group"),
        P("ctx", "group"),
        P("ctx", "group"),
        P("group", None),
    )
    return jax.shard_map(
        functools.partial(body, n_group, n_ctx // (N_XLO * N_CORE)),
        mesh=mesh, in_specs=in_specs, out_specs=P("ctx", "group"), check_vma=False,
    )
```

```python
import functools
import math

import jax
import jax.numpy as jnp
from jax import lax
from jax.experimental import pallas as pl
from jax.experimental.pallas import tpu as pltpu
from jax.sharding import PartitionSpec as P

MESH = pl.DeviceIdType.MESH
HEAD_DIM = 128
SCALING = HEAD_DIM ** (-0.5)
EXP2_SCALE = SCALING * math.log2(math.e)
N_Y, N_XLO, N_CORE = 4, 2, 2
WINDOW = 48
F32, BF16 = jnp.float32, jnp.bfloat16


def dot_nt(a, b):
    return lax.dot_general(a, b, (((1,), (1,)), ((), ())), preferred_element_type=F32)


def dot_nn(a, b):
    return lax.dot_general(a, b, (((1,), (0,)), ((), ())), preferred_element_type=F32)


def kernel(
    n_group, n_z, rows,
    q_ref, k_ref, v_ref, d_ref, w_ref, out_ref,
    kv, qd, pw, highs, high, acc, dirb, att, tbuf, tin, wbuf, plow, cout, cin, cbuf, qg, qg_out, qg_in,
    red_z, red_g, red_c, curve_sum,
    local_sem, swap_send, swap_recv, ring_send, ring_recv, sib_send, sib_recv,
    w_send, w_recv, t_send, t_recv, c_send, c_recv, red_send, red_recv, back_send, back_recv,
):
    group, ctx = lax.axis_index("group"), lax.axis_index("ctx")
    x_hi, y = lax.div(group, N_Y), lax.rem(group, N_Y)
    z, x_lo, core = lax.div(ctx, 4), lax.rem(lax.div(ctx, 2), 2), lax.rem(ctx, 2)
    head = 2 * group + x_lo
    both = 2 * rows
    unit = 4 * rows
    half_z = n_z // 2
    n_heads = 2 * n_group
    wide = wbuf.shape[1]

    def at_ctx(z_, x_lo_, core_):
        return 4 * z_ + 2 * x_lo_ + core_

    z_next, z_prev = lax.rem(z + 1, n_z), lax.rem(z + n_z - 1, n_z)
    dev_next = (group, at_ctx(z_next, x_lo, core))
    dev_prev = (group, at_ctx(z_prev, x_lo, core))
    dev_sib = (group, at_ctx(z, x_lo, 1 - core))
    dev_pair = (group, at_ctx(z, 1 - x_lo, core))
    dev_across = ((1 - x_hi) * N_Y + y, at_ctx(z, 1 - x_lo, core))
    y_next, y_prev = lax.rem(y + 1, N_Y), lax.rem(y + N_Y - 1, N_Y)
    dev_up = (x_hi * N_Y + y_next, ctx)
    dev_down = (x_hi * N_Y + y_prev, ctx)

    def remote(src, dst, send, recv, device):
        return pltpu.make_async_remote_copy(
            src_ref=src, dst_ref=dst, send_sem=send, recv_sem=recv,
            device_id=device, device_id_type=MESH,
        )

    def part_of(o):
        return x_lo + o - 2 * x_lo * o

    def chunk_rows(p, core_, j):
        start = lax.div(p, 2) * (2 * unit) + j * unit + lax.rem(p, 2) * both + core_ * rows
        return pl.ds(pl.multiple_of(start, 16), rows)

    def chunk(p, core_, j):
        return kv.at[chunk_rows(p, core_, j)]

    own_cols = pl.ds(pl.multiple_of(x_lo * HEAD_DIM, HEAD_DIM), HEAD_DIM)
    other_cols = pl.ds(pl.multiple_of((1 - x_lo) * HEAD_DIM, HEAD_DIM), HEAD_DIM)
    own_rows = pl.ds(pl.multiple_of(x_lo * rows, 16), rows)
    other_rows = pl.ds(pl.multiple_of((1 - x_lo) * rows, 16), rows)
    own_tan = pl.ds(pl.multiple_of(both + x_lo * rows, 16), rows)
    other_tan = pl.ds(pl.multiple_of(both + (1 - x_lo) * rows, 16), rows)
    first = chunk_rows(0, core, x_lo)
    second = chunk_rows(0, core, 1 - x_lo)
    own_half = pl.ds(pl.multiple_of(x_lo * wide, 128), wide)
    other_half = pl.ds(pl.multiple_of((1 - x_lo) * wide, 128), wide)

    def w_rows(x_hi_, y_, piece):
        start = (x_hi_ * N_Y + y_) * 256 + piece * 128
        return pl.ds(pl.multiple_of(start, 128), 128)

    local = [
        pltpu.make_async_copy(k_ref.at[:, own_cols], kv.at[first, 0:HEAD_DIM], local_sem.at[0]),
        pltpu.make_async_copy(
            v_ref.at[:, own_cols], kv.at[first, HEAD_DIM : 2 * HEAD_DIM], local_sem.at[1]
        ),
        pltpu.make_async_copy(q_ref.at[:, own_cols], qd.at[own_rows], local_sem.at[2]),
        pltpu.make_async_copy(d_ref.at[:, own_cols], qd.at[own_tan], local_sem.at[3]),
        pltpu.make_async_copy(d_ref, dirb, local_sem.at[4]),
        pltpu.make_async_copy(
            w_ref.at[:, own_half],
            wbuf.at[pl.ds(pl.multiple_of(group * 256, 256), 256)],
            local_sem.at[5],
        ),
    ]
    for copy in local:
        copy.start()

    barrier = pltpu.get_barrier_semaphore()

    def greet(device):
        pl.semaphore_signal(barrier, inc=1, device_id=device, device_id_type=MESH)

    greet(dev_next)
    greet(dev_prev)
    greet(dev_sib)
    greet(dev_pair)
    greet(dev_up)
    greet(dev_down)
    greet(dev_across)
    pl.semaphore_wait(barrier, 7)

    swap = [
        remote(
            k_ref.at[:, other_cols], kv.at[first, 0:HEAD_DIM],
            swap_send.at[0], swap_recv.at[0], dev_pair,
        ),
        remote(
            v_ref.at[:, other_cols], kv.at[first, HEAD_DIM : 2 * HEAD_DIM],
            swap_send.at[1], swap_recv.at[1], dev_pair,
        ),
        remote(
            q_ref.at[:, other_cols], qd.at[own_rows], swap_send.at[2], swap_recv.at[2], dev_pair
        ),
        remote(
            d_ref.at[:, other_cols], qd.at[own_tan], swap_send.at[3], swap_recv.at[3], dev_pair
        ),
    ]
    swap_in = [
        remote(
            k_ref.at[:, other_cols], kv.at[second, 0:HEAD_DIM],
            swap_send.at[0], swap_recv.at[0], dev_pair,
        ),
        remote(
            v_ref.at[:, other_cols], kv.at[second, HEAD_DIM : 2 * HEAD_DIM],
            swap_send.at[1], swap_recv.at[1], dev_pair,
        ),
        remote(
            q_ref.at[:, other_cols], qd.at[other_rows], swap_send.at[2], swap_recv.at[2], dev_pair
        ),
        remote(
            d_ref.at[:, other_cols], qd.at[other_tan], swap_send.at[3], swap_recv.at[3], dev_pair
        ),
    ]
    swap[0].start()
    swap[1].start()

    def ring(way, s, o, f, src_p, dst_p):
        j = part_of(o)
        cols = slice(f * HEAD_DIM, (f + 1) * HEAD_DIM)
        return remote(
            kv.at[chunk_rows(src_p, core, j), cols], kv.at[chunk_rows(dst_p, core, j), cols],
            ring_send.at[way, s - 1, o, f], ring_recv.at[way, s - 1, o, f],
            dev_next if way == 0 else dev_prev,
        )

    def sibling(p, o, core_):
        place = chunk(p, core_, part_of(o))
        return remote(place, place, sib_send.at[p, o], sib_recv.at[p, o], dev_sib)

    for f in range(2):
        for way in range(2):
            remote(
                (k_ref, v_ref)[f].at[:, own_cols],
                kv.at[chunk_rows(1 + way, core, x_lo), f * HEAD_DIM : (f + 1) * HEAD_DIM],
                ring_send.at[way, 0, 0, f], ring_recv.at[way, 0, 0, f],
                dev_prev if way else dev_next,
            ).start()
    swap[2].start()
    swap[3].start()
    local[0].wait()
    local[1].wait()
    sibling(0, 0, core).start()

    def w_copy(n, src, dst, device):
        return remote(src, dst, w_send.at[n], w_recv.at[n], device)

    def w_piece(x_hi_, y_, piece):
        return wbuf.at[w_rows(x_hi_, y_, piece)]

    def w_half(x_hi_, y_, part):
        start = (x_hi_ * N_Y + y_) * 256 + core * 128 + part * 64
        return wbuf.at[pl.ds(pl.multiple_of(start, 64), 64)]

    own_w = w_piece(x_hi, y, core)
    across_w = w_piece(1 - x_hi, y, core)
    y_far = lax.rem(y + 2, N_Y)
    w_src = w_ref.at[pl.ds(pl.multiple_of(core * 128, 128), 128), other_half]
    local[5].wait()
    w_copy(0, w_src, own_w, dev_across).start()
    w_copy(1, own_w, own_w, dev_up).start()
    w_copy(2, own_w, own_w, dev_down).start()

    for f in range(2):
        swap_in[f].wait_recv()
        ring(0, 1, 1, f, 0, 1).start()
        ring(1, 1, 1, f, 0, 2).start()
    sibling(0, 1, core).start()

    def w_sibling(n, x_hi_, y_, core_):
        place = w_piece(x_hi_, y_, core_)
        return w_copy(n, place, place, dev_sib)

    def w_middle():
        w_copy(0, across_w, across_w, dev_across).wait_recv()
        w_copy(5, across_w, across_w, dev_up).start()
        w_copy(6, across_w, across_w, dev_down).start()
        below, above = w_piece(x_hi, y_prev, core), w_piece(x_hi, y_next, core)
        w_copy(1, below, below, dev_up).wait_recv()
        onward = w_half(x_hi, y_prev, 0)
        w_copy(3, onward, onward, dev_up).start()
        w_copy(2, above, above, dev_down).wait_recv()
        onward = w_half(x_hi, y_next, 1)
        w_copy(4, onward, onward, dev_down).start()
        w_sibling(9, 1 - x_hi, y, core).start()
        w_sibling(10, x_hi, y_prev, core).start()
        w_sibling(11, x_hi, y_next, core).start()

    def w_late():
        below, above = w_piece(1 - x_hi, y_prev, core), w_piece(1 - x_hi, y_next, core)
        w_copy(5, below, below, dev_up).wait_recv()
        onward = w_half(1 - x_hi, y_prev, 0)
        w_copy(7, onward, onward, dev_up).start()
        w_copy(6, above, above, dev_down).wait_recv()
        onward = w_half(1 - x_hi, y_next, 1)
        w_copy(8, onward, onward, dev_down).start()
        w_sibling(13, 1 - x_hi, y_prev, core).start()
        w_sibling(14, 1 - x_hi, y_next, core).start()
        place = w_half(x_hi, y_far, 0)
        w_copy(3, place, place, dev_up).wait_recv()
        place = w_half(x_hi, y_far, 1)
        w_copy(4, place, place, dev_down).wait_recv()
        w_sibling(12, x_hi, y_far, core).start()

    def w_sent():
        for copy in swap:
            copy.wait_send()
        for n in (0, 1, 2, 5, 6):
            w_copy(n, own_w, own_w, dev_up).wait_send()
        for n in (3, 4):
            w_copy(n, w_half(x_hi, y, 0), w_half(x_hi, y, 0), dev_up).wait_send()
        for n in range(9, 15):
            w_sibling(n, x_hi, y, core).wait_send()

    def w_last():
        place = w_half(1 - x_hi, y_far, 0)
        w_copy(7, place, place, dev_up).wait_recv()
        place = w_half(1 - x_hi, y_far, 1)
        w_copy(8, place, place, dev_down).wait_recv()
        w_sibling(15, 1 - x_hi, y_far, core).start()

    def w_finish():
        w_sibling(9, 1 - x_hi, y, 1 - core).wait_recv()
        w_sibling(10, x_hi, y_prev, 1 - core).wait_recv()
        w_sibling(11, x_hi, y_next, 1 - core).wait_recv()
        w_sibling(12, x_hi, y_far, 1 - core).wait_recv()
        w_sibling(13, 1 - x_hi, y_prev, 1 - core).wait_recv()
        w_sibling(14, 1 - x_hi, y_next, 1 - core).wait_recv()
        w_sibling(15, 1 - x_hi, y_far, 1 - core).wait_recv()

    high[...] = jnp.full(high.shape, -1e30, F32)
    acc[...] = jnp.zeros(acc.shape, F32)
    qg[...] = jnp.zeros(qg.shape, F32)
    def service(h):
        b, o = lax.div(h, 2), lax.rem(h, 2)
        s = b + 1
        back_p, ahead_p = 2 * s - 1, 2 * s

        @pl.when(s + 1 < half_z)
        def _():
            for f in range(2):
                ring(0, s, o, f, back_p, back_p).wait_recv()
                ring(0, s + 1, o, f, back_p, back_p + 2).start()
                ring(1, s, o, f, ahead_p, ahead_p).wait_recv()
                ring(1, s + 1, o, f, ahead_p, ahead_p + 2).start()

        @pl.when(s + 1 == half_z)
        def _():
            for f in range(2):
                ring(0, s, o, f, back_p, back_p).wait_recv()

                @pl.when(o == 0)
                def _():
                    ring(0, s + 1, o, f, back_p, back_p + 2).start()

                ring(1, s, o, f, ahead_p, ahead_p).wait_recv()

                @pl.when(o == 1)
                def _():
                    ring(1, s + 1, o, f, ahead_p, n_z - 1).start()

        @pl.when(s < half_z)
        def _():
            sibling(back_p, o, core).start()
            sibling(ahead_p, o, core).start()

        @pl.when(s == half_z)
        def _():
            for f in range(2):

                @pl.when(o == 0)
                def _():
                    ring(0, s, o, f, back_p, back_p).wait_recv()

                @pl.when(o == 1)
                def _():
                    ring(1, s, o, f, back_p, back_p).wait_recv()

            sibling(back_p, o, core).start()

        @pl.when(s >= 2)
        def _():
            for f in range(2):
                ring(0, s - 1, o, f, 1, 1).wait_send()
                ring(1, s - 1, o, f, 1, 1).wait_send()
            sibling(2 * s - 3, o, core).wait_send()
            sibling(2 * s - 2, o, core).wait_send()

    def unit_rows(h):
        start = lax.div(h, 2) * (2 * unit) + part_of(lax.rem(h, 2)) * unit
        return pl.ds(pl.multiple_of(start, 16), unit)

    ones = jnp.ones((unit, HEAD_DIM), BF16)

    def forward(h):
        b, o = lax.div(h, 2), lax.rem(h, 2)

        @pl.when(b == 0)
        def _():
            sibling(0, o, 1 - core).wait_recv()

        sibling(2 * b + 1, o, 1 - core).wait_recv()

        @pl.when(b + 1 < half_z)
        def _():
            sibling(2 * b + 2, o, 1 - core).wait_recv()

        here = unit_rows(h)
        keys = kv[here, 0:HEAD_DIM]
        values = kv[here, HEAD_DIM : 2 * HEAD_DIM]
        scores = dot_nt(qd[0:both], keys)
        tangents = dot_nt(qd[both : 2 * both], keys)
        old = high[...]
        new = jnp.maximum(old, jnp.max(scores, axis=1, keepdims=True))
        high[...] = new
        highs[h] = new
        factor = jnp.exp2((old - new) * EXP2_SCALE)
        weights = jnp.exp2((scores - new) * EXP2_SCALE)
        weighted = weights * tangents
        pw[h, 0:both] = weights.astype(BF16)
        pw[h, both : 2 * both] = weighted.astype(BF16)
        mixed = dot_nn(pw[h], jnp.concatenate([values, ones], axis=1))
        acc[0:both] = acc[0:both] * factor + mixed[0:both]
        acc[both : 2 * both] = acc[both : 2 * both] * factor + mixed[both : 2 * both]

    n_units = n_z
    service(0)
    for copy in local[2:5]:
        copy.wait()
    swap_in[2].wait_recv()
    swap_in[3].wait_recv()
    direction = dirb[...].astype(F32)
    squares = jnp.sum((direction * direction).reshape(rows // 8, 8, 2 * HEAD_DIM), axis=0)
    residual_part = squares[:, :HEAD_DIM] + squares[:, HEAD_DIM:]

    @pl.loop(1, n_units + 1)
    def _(h):
        @pl.when(h < n_units)
        def _():
            service(h)

        @pl.when(h == 5)
        def _():
            w_middle()

        @pl.when(h == 12)
        def _():
            w_late()

        @pl.when(h == 14)
        def _():
            w_sent()

        @pl.when(h == n_units)
        def _():
            w_last()

        forward(h - 1)

    totals = acc[0:both, HEAD_DIM : 2 * HEAD_DIM]
    attended = acc[0:both, 0:HEAD_DIM] / totals
    tbuf[...] = (
        (acc[both : 2 * both, 0:HEAD_DIM] - acc[both : 2 * both, HEAD_DIM : 2 * HEAD_DIM] * attended)
        * (SCALING / totals)
    ).astype(BF16)

    def window_start(i):
        return lax.div(((both // 16 - 3) * i + 3), n_group - 1) * 16

    def window(i):
        return pl.ds(pl.multiple_of(window_start(i), 16), WINDOW)

    def head_cols(h_):
        return pl.ds(pl.multiple_of(h_ * HEAD_DIM, HEAD_DIM), HEAD_DIM)

    def t_copy(group_, x_lo_, slot):
        return remote(
            tbuf.at[window(group_)], tin.at[:, head_cols(head)],
            t_send.at[slot], t_recv.at[head], (group_, at_ctx(z, x_lo_, core)),
        )

    def t_arrival(h_):
        return remote(
            tbuf.at[window(0)], tin.at[:, head_cols(h_)], t_send.at[0], t_recv.at[h_], dev_pair
        )

    t_copy(group, 1 - x_lo, 0).start()
    for i in sorted(range(1, n_group), key=lambda i: (0, 2, 3, 2)[i % N_Y], reverse=True):
        other = lax.rem(group + i, n_group)
        t_copy(other, x_lo, 2 * i).start()
        t_copy(other, 1 - x_lo, 2 * i + 1).start()

    tin[:, head_cols(head)] = tbuf[window(group)]
    att[...] = attended
    w_finish()

    for f in range(2):
        ring(0, half_z, 0, f, 1, 1).wait_send()
        ring(1, half_z, 1, f, 1, 1).wait_send()
    for o in range(2):
        sibling(0, o, core).wait_send()
        sibling(n_z - 1, o, core).wait_send()
    for n in (7, 8):
        w_copy(n, w_half(x_hi, y, 0), w_half(x_hi, y, 0), dev_up).wait_send()
    w_sibling(15, x_hi, y, core).wait_send()

    for i in range(1, n_heads):
        t_arrival(lax.rem(head + i, n_heads)).wait_recv()

    counted = window_start(group + 1) - window_start(group)
    row_id = lax.broadcasted_iota(jnp.int32, (WINDOW, HEAD_DIM), 0)
    step = wide // 3
    curve_sum[...] = jnp.zeros(curve_sum.shape, F32)

    @pl.loop(0, 3)
    def _(n):
        cols = pl.ds(pl.multiple_of(n * step, 128), step)
        proj = dot_nn(tin[...], wbuf[:, cols])
        plow[:, cols] = proj.astype(BF16)
        squared = proj * proj
        lanes = squared[:, 0:HEAD_DIM]
        for m in range(1, step // HEAD_DIM):
            lanes = lanes + squared[:, m * HEAD_DIM : (m + 1) * HEAD_DIM]
        lanes = jnp.where(row_id < counted, lanes, 0.0)
        curve_sum[...] += jnp.sum(lanes.reshape(WINDOW // 8, 8, HEAD_DIM), axis=0)

    red_z[z, 0:8] = curve_sum[...]
    red_z[z, 8:16] = residual_part

    def red_copy(buf, here, n, base, device):
        return remote(buf.at[here], buf.at[here], red_send.at[n], red_recv.at[base + here], device)

    def red_arrival(buf, there, base):
        return remote(buf.at[there], buf.at[there], red_send.at[0], red_recv.at[base + there], dev_pair)

    for i in sorted(range(1, n_z), key=lambda i: -min(i, n_z - i)):
        other = lax.rem(z + i, n_z)
        red_copy(red_z, z, i, 0, (group, at_ctx(other, x_lo, core))).start()

    def c_copy(h_):
        return remote(
            cout.at[:, head_cols(h_)], cin.at[x_lo, group],
            c_send.at[h_], c_recv.at[x_lo * n_group + group],
            (lax.div(h_, 2), at_ctx(z, lax.rem(h_, 2), core)),
        )

    def c_arrival(x_lo_, group_):
        return remote(
            cout.at[:, head_cols(0)], cin.at[x_lo_, group_],
            c_send.at[0], c_recv.at[x_lo_ * n_group + group_], dev_pair,
        )

    block = 512

    @pl.loop(0, n_heads * HEAD_DIM // block)
    def _(n):
        at = pl.ds(pl.multiple_of(n * block, block), block)
        cout[:, at] = dot_nt(plow[...], wbuf[at]).astype(BF16)

        for i in range(block // HEAD_DIM):
            h_ = n * (block // HEAD_DIM) + i

            @pl.when(h_ != head)
            def _():
                c_copy(h_).start()

    cin[x_lo, group] = cout[:, head_cols(head)]

    t_copy(group, 1 - x_lo, 0).wait_send()
    for i in range(2, n_heads):
        t_copy(0, 0, i).wait_send()

    for i in range(1, n_group):
        c_arrival(x_lo, lax.rem(group + i, n_group)).wait_recv()
    for i in range(n_group):
        c_arrival(1 - x_lo, i).wait_recv()

    starts = [((both // 16 - 3) * i + 3) // (n_group - 1) * 16 for i in range(n_group)]
    for i in range(n_group):
        cbuf[starts[i] : starts[i] + WINDOW] = (
            cin[0, i].astype(F32) + cin[1, i].astype(F32)
        ).astype(BF16)

    def backward(first_unit, block_rows):
        cot = cbuf[block_rows]
        centering = jnp.sum(cot.astype(F32) * att[block_rows], axis=1, keepdims=True)
        final = high[block_rows]
        units = [first_unit + i for i in range(4)]
        backs = [dot_nt(cot, kv[unit_rows(h), HEAD_DIM : 2 * HEAD_DIM]) for h in units]
        total = None
        for h, back in zip(units, backs):
            grad = (pw[h, block_rows].astype(F32) * (back - centering)).astype(BF16)
            factor = jnp.exp2((highs[h, block_rows] - final) * EXP2_SCALE)
            product = dot_nn(grad, kv[unit_rows(h), 0:HEAD_DIM]) * factor
            total = product if total is None else total + product
        qg[block_rows] += total

    def scaled(block_rows):
        return qg[block_rows] * (SCALING / acc[block_rows, HEAD_DIM : 2 * HEAD_DIM])

    back_copy = remote(qg_out, qg_in, back_send.at[0], back_recv.at[0], dev_pair)
    last = red_copy(red_c, core, n_z + n_heads, n_z + n_heads, dev_sib)
    per_half = n_units // 4

    for i in range(1, n_z):
        red_arrival(red_z, lax.rem(z + i, n_z), 0).wait_recv()
    red_g[head] = jnp.sum(red_z[...], axis=0)
    for i in sorted(range(1, n_heads), key=lambda i: (0, 2, 3, 2)[i // 2 % N_Y], reverse=True):
        other = lax.rem(head + i, n_heads)
        device = (lax.div(other, 2), at_ctx(z, lax.rem(other, 2), core))
        red_copy(red_g, head, n_z + i, n_z, device).start()

    @pl.loop(0, 2 * per_half)
    def _(i):
        mine = lax.div(i, per_half)
        side = 1 - x_lo + mine * (2 * x_lo - 1)
        backward(
            4 * (i - mine * per_half), pl.ds(pl.multiple_of(side * rows, 16), rows)
        )

        @pl.when(i == per_half - 1)
        def _():
            qg_out[...] = scaled(other_rows).astype(BF16)
            back_copy.start()

        @pl.when(i == 2 * per_half - 2)
        def _():
            for i in range(1, n_heads):
                red_arrival(red_g, lax.rem(head + i, n_heads), n_z).wait_recv()
            red_c[core] = jnp.sum(red_g[...], axis=0)
            last.start()

    for i in range(1, n_z):
        red_copy(red_z, z, i, 0, dev_next).wait_send()
    for i in range(1, n_heads):
        red_copy(red_g, head, n_z + i, n_z, dev_pair).wait_send()
    for h_ in range(n_heads):

        @pl.when(h_ != head)
        def _():
            c_copy(h_).wait_send()

    red_arrival(red_c, 1 - core, n_z + n_heads).wait_recv()
    last.wait_send()
    sums = jnp.sum(red_c[...], axis=0)
    curvature = jnp.sum(jnp.sum(sums[0:8], axis=0, keepdims=True), axis=1, keepdims=True)
    residual_sq = jnp.sum(jnp.sum(sums[8:16], axis=0, keepdims=True), axis=1, keepdims=True)
    step_size = residual_sq / curvature
    out_ref[:, own_cols] = dirb[:, own_cols].astype(F32) - step_size * scaled(own_rows)
    back_copy.wait_recv()
    out_ref[:, other_cols] = dirb[:, other_cols].astype(F32) - step_size * qg_in[...].astype(F32)
    back_copy.wait_send()


def body(n_group, n_z, queries, key_rows, value_rows, query_dir, out_weight):
    rows = queries.shape[0]
    both, unit = 2 * rows, 4 * rows
    width = out_weight.shape[1]
    n_heads = 2 * n_group
    any_spec = pl.BlockSpec(memory_space=pl.ANY)
    dma = pltpu.SemaphoreType.DMA
    n_red = n_z + n_heads + 2
    return pl.pallas_call(
        functools.partial(kernel, n_group, n_z, rows),
        out_shape=jax.ShapeDtypeStruct((rows, 2 * HEAD_DIM), F32),
        in_specs=[any_spec] * 5,
        out_specs=pl.BlockSpec(memory_space=pltpu.VMEM),
        scratch_shapes=[
            pltpu.VMEM((n_z * unit, 2 * HEAD_DIM), BF16),
            pltpu.VMEM((2 * both, HEAD_DIM), BF16),
            pltpu.VMEM((n_z, 2 * both, unit), BF16),
            pltpu.VMEM((n_z, both, 1), F32),
            pltpu.VMEM((both, 1), F32),
            pltpu.VMEM((2 * both, 2 * HEAD_DIM), F32),
            pltpu.VMEM((rows, 2 * HEAD_DIM), BF16),
            pltpu.VMEM((both, HEAD_DIM), F32),
            pltpu.VMEM((both, HEAD_DIM), BF16),
            pltpu.VMEM((WINDOW, n_heads * HEAD_DIM), BF16),
            pltpu.VMEM((n_heads * HEAD_DIM, width // 2), BF16),
            pltpu.VMEM((WINDOW, width // 2), BF16),
            pltpu.VMEM((WINDOW, n_heads * HEAD_DIM), BF16),
            pltpu.VMEM((2, n_group, WINDOW, HEAD_DIM), BF16),
            pltpu.VMEM((both, HEAD_DIM), BF16),
            pltpu.VMEM((both, HEAD_DIM), F32),
            pltpu.VMEM((rows, HEAD_DIM), BF16),
            pltpu.VMEM((rows, HEAD_DIM), BF16),
            pltpu.VMEM((n_z, 16, HEAD_DIM), F32),
            pltpu.VMEM((n_heads, 16, HEAD_DIM), F32),
            pltpu.VMEM((2, 16, HEAD_DIM), F32),
            pltpu.VMEM((8, HEAD_DIM), F32),
            dma((6,)),
            dma((4,)), dma((4,)),
            dma((2, n_z // 2, 2, 2)), dma((2, n_z // 2, 2, 2)),
            dma((n_z, 2)), dma((n_z, 2)),
            dma((16,)), dma((16,)),
            dma((n_heads,)), dma((n_heads,)),
            dma((n_heads,)), dma((n_heads,)),
            dma((n_red,)), dma((n_red,)),
            dma((1,)), dma((1,)),
        ],
        compiler_params=pltpu.CompilerParams(
            collective_id=0, has_side_effects=True, vmem_limit_bytes=60 * 1024 * 1024
        ),
        name="gauss_newton_layer",
    )(queries, key_rows, value_rows, query_dir, out_weight)


def solution(mesh):
    n_group, n_ctx = mesh.shape["group"], mesh.shape["ctx"]
    in_specs = (
        P("ctx", "group"),
        P("ctx", "group"),
        P("ctx", "group"),
        P("ctx", "group"),
        P("group", None),
    )
    return jax.shard_map(
        functools.partial(body, n_group, n_ctx // (N_XLO * N_CORE)),
        mesh=mesh, in_specs=in_specs, out_specs=P("ctx", "group"), check_vma=False,
    )
```
